32 devices in a mesh: dp: 8 (over z, x), head: 4 (over y, core).
Axes of the slice: x: 2, y: 2, z: 4, core: 2. Of those that a mesh axis runs over, the one named last changes fastest.
Arguments:
- q_raw: bfloat16 [12288, 2560], P('dp', 'head'), may hold values from -2000 to 2000
- k_raw: bfloat16 [12288, 512], P('dp', 'head'), may hold values from -2000 to 2000
- v_proj: bfloat16 [12288, 512], P('dp', 'head'), may hold values from -6 to 6
- d_out: bfloat16 [12288, 2560], P('dp', 'head'), may hold values from -6 to 6
- q_gain: float32 [2560], P('head'), may hold values from 0.5 to 2
- k_gain: float32 [512], P('head'), may hold values from 0.5 to 2
- doc_lengths: int32 [8, 8], P('dp'), may hold values from 1 to 384, as said below
- plan_dest: int32 [8, 8], P('dp'), may hold values from 0 to 7, as said below
- plan_offset: int32 [8, 8], P('dp'), may hold values from 0 to 192, as said below
Outputs:
- grad_q: bfloat16 [12288, 2560], P('dp', 'head')
- grad_k: bfloat16 [12288, 512], P('dp', 'head')
- grad_v: bfloat16 [12288, 512], P('dp', 'head')
- balanced_lse: float32 [20, 27648], P('head', 'dp')
The draws below stay inside these ranges and needn't reach their ends.
Inputs may be any that keep to these rules, and one draw needn't show every extreme that they name: `doc_lengths`: each row holds the lengths of one sequence's documents in order and sums to 1536; the largest and the smallest length are reached in every draw. In each row exactly 4 documents have a plan_dest other than the row's own device, no two of them the same device; each of them has 192 to 384 rows, and in every row one has exactly 384 rows and one exactly 192. The documents that keep the row's own device sum to exactly 384 tokens. For a document sent to another device, plan_offset plus its length is at most 384; documents that stay have 0. Every row reaches the largest value.
All inputs are finite; a program needn't handle non-finite values.
Results may differ from the reference program's by a relative error of at most 0.008.
The reference program's roundings to bfloat16 on the way (of `q_norm`, `k_norm`, `weights_low`, `grad_scores`, `dq_norm` and `dk_norm`) count: a program that leaves them out, or rounds other values in their place, can miss the bound.
Values may be sent and summed in bfloat16 or wider, within the bound.
A program may use at most 128 MiB of HBM per device.

```python
import math
from functools import partial
import jax
import jax.numpy as jnp
from jax import lax

HEADS = 20
KV_HEADS = 4
HDIM = 128
TOK_DEV = 1536
KEEP = 4
HOME = 384
SLOT = 384
MOVED = 4
DOCS = 8
TOKENS = 12288
QW = 2560
KW = 512
BALANCED = 27648
N_DP = 8


def plan_layout(key):
    chooser = jax.random.fold_in(key, 5)
    heavy = jax.random.permutation(chooser, N_DP) < N_DP // 4
    quarter = SLOT // 4
    half_pairs = MOVED // 2
    eighth = HOME // 8
    part_len = HOME // 4

    def one_source(index):
        inner = jax.random.fold_in(jax.random.fold_in(key, 9), index)
        streams = jax.random.split(inner, 5)
        spread = jax.random.randint(streams[0], (half_pairs,), 0, quarter + 1).astype(jnp.int32)
        spread = spread.at[0].set(quarter)
        moved_len = jnp.stack([3 * quarter + spread, 3 * quarter - spread], axis=1).reshape(MOVED).astype(jnp.int32)
        moved_shift = (jax.random.randint(streams[1], (MOVED,), 0, SLOT + 1) % (SLOT - moved_len + 1)).astype(jnp.int32)
        moved_shift = moved_shift.at[1].set(SLOT // 2)
        jitter = jax.random.randint(streams[2], (2,), 0, eighth + 1).astype(jnp.int32)
        light_len = jnp.stack([part_len + jitter[0], part_len - jitter[0], part_len + jitter[1], part_len - jitter[1]]).astype(jnp.int32)
        heavy_len = jnp.array([HOME - 3, 1, 1, 1], jnp.int32)
        keep_len = jnp.where(heavy[index], heavy_len, light_len).astype(jnp.int32)
        everyone = jnp.arange(N_DP, dtype=jnp.int32)
        avoid = (heavy & heavy[index]).astype(jnp.int32)
        ranking = jax.random.permutation(streams[3], N_DP).astype(jnp.int32) + N_DP * avoid + 2 * N_DP * (everyone == index).astype(jnp.int32)
        moved_dest = jnp.argsort(ranking)[:MOVED].astype(jnp.int32)
        lengths = jnp.concatenate([moved_len, keep_len])
        targets = jnp.concatenate([moved_dest, jnp.full((KEEP,), index, jnp.int32)])
        shifts = jnp.concatenate([moved_shift, jnp.zeros((KEEP,), jnp.int32)])
        order = jax.random.permutation(streams[4], DOCS)
        return (lengths[order], targets[order], shifts[order])
    return jax.vmap(one_source)(jnp.arange(N_DP, dtype=jnp.int32))


def draw_doc_lengths(key, part):
    layout = plan_layout(key)
    return layout[0]


def draw_plan_dest(key, part):
    layout = plan_layout(key)
    return layout[1]


def draw_plan_offset(key, part):
    layout = plan_layout(key)
    return layout[2]


def spread_scales(key, rows, width):
    first, second = jax.random.split(key)
    row_scale = jnp.exp(jax.random.uniform(first, (rows, 1), jnp.float32, 0.0, math.log(10.0)))
    rising = jnp.exp(jnp.arange(width, dtype=jnp.float32) * (math.log(3.0) / width))
    col_scale = jnp.exp(jax.random.uniform(second, (1, width), jnp.float32, 0.0, math.log(10.0))) * rising[None, :]
    return row_scale * col_scale


def draw_q_raw(key, part):
    key = jax.random.fold_in(key, 11)
    streams = jax.random.split(key, 2)
    width = HEADS * HDIM
    scales = spread_scales(streams[0], TOKENS, width)
    values = jnp.clip(jax.random.normal(streams[1], (TOKENS, width), jnp.float32), -6.0, 6.0) * scales
    return values.astype(jnp.bfloat16)


def draw_k_raw(key, part):
    key = jax.random.fold_in(key, 13)
    streams = jax.random.split(key, 2)
    width = KV_HEADS * HDIM
    scales = spread_scales(streams[0], TOKENS, width)
    values = jnp.clip(jax.random.normal(streams[1], (TOKENS, width), jnp.float32), -6.0, 6.0) * scales
    return values.astype(jnp.bfloat16)


def block_levels(rng, dims, cuts, low, high):
    loudness, own = 1.0, jax.random.fold_in(rng, 6)
    for axis_at, blocks in cuts:
        steps = jnp.exp(jax.random.uniform(jax.random.fold_in(own, axis_at), (blocks,), jnp.float32, low / len(cuts), high / len(cuts)))
        loudness = loudness * jnp.repeat(steps, dims[axis_at] // blocks).reshape([-1 if axis == axis_at else 1 for axis in range(len(dims))])
    return loudness


def bell_draw(rng, extent, scale, reach, cuts=(), kind=jnp.bfloat16):
    result = jax.random.normal(rng, extent, jnp.float32) * scale
    if len(cuts) > 0:
        result = block_levels(rng, extent, cuts, -0.22, 0.18) * result
    return jnp.clip(result, min=-reach, max=reach).astype(kind)


def setup_inputs(seed: int = 0) -> dict:
    key_of = jax.random.split(jax.random.key(seed), 10)
    q_raw = draw_q_raw(jax.random.fold_in(key_of[9], 71), 0)
    k_raw = draw_k_raw(jax.random.fold_in(key_of[9], 71), 0)
    v_proj = bell_draw(key_of[2], (TOKENS, KW), 1.0, 6.0, ((0, 8), (1, 4)))
    d_out = bell_draw(key_of[3], (TOKENS, QW), 1.0, 6.0, ((0, 8), (1, 4)))
    q_gain = jnp.clip(jnp.exp(math.log(2.0) - 1.3862944 * jax.random.uniform(key_of[4], (QW,), jnp.float32) ** block_levels(key_of[4], (QW,), ((0, 4),), -0.2, 0.2)), 0.5, 2.0)
    k_gain = jnp.clip(jnp.exp(math.log(2.0) - 1.3862944 * jax.random.uniform(key_of[5], (KW,), jnp.float32) ** block_levels(key_of[5], (KW,), ((0, 4),), -0.2, 0.2)), 0.5, 2.0)
    doc_lengths = draw_doc_lengths(jax.random.fold_in(key_of[9], 71), 0)
    plan_dest = draw_plan_dest(jax.random.fold_in(key_of[9], 71), 0)
    plan_offset = draw_plan_offset(jax.random.fold_in(key_of[9], 71), 0)
    return dict(q_raw=q_raw, k_raw=k_raw, v_proj=v_proj, d_out=d_out, q_gain=q_gain, k_gain=k_gain, doc_lengths=doc_lengths, plan_dest=plan_dest, plan_offset=plan_offset)


eps = 1e-06
big_negative = -1e+30

def rows_of_docs(doc_lengths):
    ends = jnp.cumsum(doc_lengths, axis=1).astype(jnp.int32)
    starts = (ends - doc_lengths).astype(jnp.int32)
    row_index = jnp.arange(TOK_DEV, dtype=jnp.int32)
    row_doc = lax.optimization_barrier(jnp.sum((row_index[None, :, None] >= ends[:, None, :]).astype(jnp.int32), axis=2)).astype(jnp.int32)
    return (starts, row_doc)

def one_sequence(inputs, q_gain, k_gain):
    q_raw, k_raw, v_proj, d_out, row_doc = inputs
    group_size = HEADS // KV_HEADS
    q_float = q_raw.astype(jnp.float32)
    k_float = k_raw.astype(jnp.float32)
    recip_q = lax.rsqrt(lax.optimization_barrier(jnp.mean(q_float * q_float, axis=1)) + eps)
    recip_k = lax.rsqrt(lax.optimization_barrier(jnp.mean(k_float * k_float, axis=1)) + eps)
    q_norm = lax.optimization_barrier((q_float * recip_q[:, None] * q_gain[None, :]).astype(jnp.bfloat16)).astype(jnp.float32)
    k_norm = lax.optimization_barrier((k_float * recip_k[:, None] * k_gain[None, :]).astype(jnp.bfloat16)).astype(jnp.float32)
    queries = q_norm.reshape(TOK_DEV, KV_HEADS, group_size, HDIM)
    key_heads = k_norm.reshape(TOK_DEV, KV_HEADS, HDIM)
    value_heads = v_proj.astype(jnp.float32).reshape(TOK_DEV, KV_HEADS, HDIM)
    upstream = d_out.astype(jnp.float32).reshape(TOK_DEV, KV_HEADS, group_size, HDIM)
    scaling = 1.0 / math.sqrt(HDIM)
    row_index = jnp.arange(TOK_DEV, dtype=jnp.int32)
    allowed = (row_doc[:, None] == row_doc[None, :]) & (row_index[None, :] <= row_index[:, None])
    scores = jnp.einsum('qgjd,kgd->gjqk', queries, key_heads) * scaling
    masked = jnp.where(allowed, scores, big_negative)
    row_peak = lax.optimization_barrier(jnp.max(masked, axis=-1, keepdims=True))
    row_total = lax.optimization_barrier(jnp.sum(jnp.where(allowed, jnp.exp(masked - row_peak), 0.0), axis=-1, keepdims=True))
    log_sums = row_peak + jnp.log(row_total)
    weights = jnp.where(allowed, jnp.exp(masked - log_sums), 0.0)
    weights_low = lax.optimization_barrier(weights.astype(jnp.bfloat16)).astype(jnp.float32)
    output = jnp.einsum('gjqk,kgd->qgjd', weights_low, value_heads)
    row_delta = jnp.transpose(lax.optimization_barrier(jnp.sum(upstream * output, axis=-1)), (1, 2, 0))[..., None]
    grad_values = jnp.einsum('gjqk,qgjd->kgd', weights_low, upstream)
    grad_weights = jnp.einsum('qgjd,kgd->gjqk', upstream, value_heads)
    grad_scores = weights * (grad_weights - row_delta) * scaling
    grad_low = lax.optimization_barrier(grad_scores.astype(jnp.bfloat16)).astype(jnp.float32)
    grad_query = jnp.einsum('gjqk,kgd->qgjd', grad_low, key_heads).reshape(TOK_DEV, -1)
    grad_keys = jnp.einsum('gjqk,qgjd->kgd', grad_low, queries).reshape(TOK_DEV, -1)
    dq_norm = lax.optimization_barrier(grad_query.astype(jnp.bfloat16)).astype(jnp.float32)
    dk_norm = lax.optimization_barrier(grad_keys.astype(jnp.bfloat16)).astype(jnp.float32)
    grad_v = grad_values.reshape(TOK_DEV, -1).astype(jnp.bfloat16)
    scaled_q = dq_norm * q_gain[None, :]
    back_q = lax.optimization_barrier(jnp.mean(scaled_q * q_float, axis=1))
    grad_q = (recip_q[:, None] * scaled_q - q_float * (recip_q ** 3 * back_q)[:, None]).astype(jnp.bfloat16)
    scaled_k = dk_norm * k_gain[None, :]
    back_k = lax.optimization_barrier(jnp.mean(scaled_k * k_float, axis=1))
    grad_k = (recip_k[:, None] * scaled_k - k_float * (recip_k ** 3 * back_k)[:, None]).astype(jnp.bfloat16)
    return (grad_q, grad_k, grad_v, log_sums[..., 0].reshape(HEADS, TOK_DEV))

def per_sequence(array):
    return array.reshape(N_DP, TOK_DEV, array.shape[1])

def reference(q_raw, k_raw, v_proj, d_out, q_gain, k_gain, doc_lengths, plan_dest, plan_offset):
    starts, row_doc = rows_of_docs(doc_lengths)
    worker = partial(one_sequence, q_gain=q_gain, k_gain=k_gain)
    grad_q, grad_k, grad_v, log_all = lax.map(worker, (per_sequence(q_raw), per_sequence(k_raw), per_sequence(v_proj), per_sequence(d_out), row_doc))
    row_dest = jnp.take_along_axis(plan_dest, row_doc, axis=1).astype(jnp.int32)
    row_start = jnp.take_along_axis(starts, row_doc, axis=1).astype(jnp.int32)
    row_shift = jnp.take_along_axis(plan_offset, row_doc, axis=1).astype(jnp.int32)
    source = jnp.arange(N_DP, dtype=jnp.int32)[:, None]
    position = jnp.arange(TOK_DEV, dtype=jnp.int32)[None, :]
    width_dev = HOME + 2 * TOK_DEV
    stay = row_dest == source
    rank = (jnp.cumsum(stay.astype(jnp.int32), axis=1) - 1).astype(jnp.int32)
    stay_column = source * width_dev + rank
    away_column = row_dest * width_dev + HOME + source * SLOT + row_shift + position - row_start
    target = jnp.where(stay, stay_column, away_column).astype(jnp.int32)
    flat = jnp.transpose(log_all, (1, 0, 2)).reshape(HEADS, TOKENS)
    balanced = jnp.zeros((HEADS, BALANCED), jnp.float32).at[:, target.reshape(-1)].set(flat)
    return (grad_q.reshape(TOKENS, -1), grad_k.reshape(TOKENS, -1), grad_v.reshape(TOKENS, -1), balanced)
```

```python
import functools
import math

import jax
import jax.numpy as jnp
from jax import lax
from jax.experimental import pallas as pl
from jax.experimental.pallas import tpu as pltpu
from jax.sharding import PartitionSpec as P

HDIM = 128
ROWS = 128
REACH = 384

eps = 1e-06
big_negative = -1e30


def column(row):
    return jnp.transpose(jnp.broadcast_to(row, (ROWS, ROWS)))


def row_sums(tile):
    return jnp.sum(jnp.transpose(tile), axis=0, keepdims=True)


def nt_dot(a, b):
    return lax.dot_general(a, b, (((1,), (1,)), ((), ())), preferred_element_type=jnp.float32)


def attention_kernel(
    docs,
    devices,
    slot,
    home_count,
    len_ref,
    dest_ref,
    off_ref,
    q_ref,
    grad_ref,
    k_ref,
    v_ref,
    recip_q_ref,
    recip_k_ref,
    q_gain_ref,
    k_gain_ref,
    dq_ref,
    dk_ref,
    dv_ref,
    back_ref,
    home_ref,
    slots_ref,
    kn_ref,
    kn_t_ref,
    dk_acc,
    dv_acc,
    lse_ref,
):
    step = pl.program_id(0)
    seq_len = k_ref.shape[0]
    blocks = seq_len // ROWS
    heads = q_ref.shape[1] // HDIM
    scaling = 1.0 / math.sqrt(HDIM)
    here = lax.axis_index("dp")

    @pl.when(step == 0)
    def _():
        dk_acc[...] = jnp.zeros_like(dk_acc)
        dv_acc[...] = jnp.zeros_like(dv_acc)
        lse_ref[...] = jnp.zeros_like(lse_ref)
        for b in range(blocks):
            at = slice(b * ROWS, (b + 1) * ROWS)
            normed = (
                k_ref[at, :].astype(jnp.float32)
                * column(recip_k_ref[b : b + 1, :])
                * k_gain_ref[...]
            )
            low = normed.astype(jnp.bfloat16)
            kn_ref[at, :] = low
            kn_t_ref[:, at] = jnp.transpose(low.astype(jnp.float32)).astype(jnp.bfloat16)

    base = step * ROWS
    token = base + lax.broadcasted_iota(jnp.int32, (1, ROWS), 1)
    start = jnp.zeros((1, ROWS), jnp.int32)
    first = jnp.int32(0)
    end = jnp.int32(0)
    for j in range(docs):
        end = end + len_ref[0, j]
        start = jnp.where(token >= end, end, start)
        first = jnp.where(base >= end, end, first)
    needed = step - first // ROWS + 1

    def block(count):
        width = count * ROWS
        key_at = pl.multiple_of((step - (count - 1)) * ROWS, ROWS)
        window = pl.ds(key_at, width)
        recip = column(recip_q_ref[pl.ds(step, 1), :])
        normed, upstream = [], []
        for h in range(heads):
            lanes = slice(h * HDIM, (h + 1) * HDIM)
            tile = q_ref[:, lanes].astype(jnp.float32) * recip * q_gain_ref[:, lanes]
            normed.append(tile.astype(jnp.bfloat16))
            upstream.append(grad_ref[:, lanes])
        queries = jnp.concatenate(normed, axis=0)
        grads = jnp.concatenate(upstream, axis=0)
        scores = nt_dot(kn_ref[window, :], queries)
        grad_weights = nt_dot(v_ref[window, :], grads)
        key = key_at + lax.broadcasted_iota(jnp.int32, (width, ROWS), 0)
        bias = jnp.where((key >= start) & (key <= token), 0.0, big_negative)
        weights_all, grad_all = [], []
        for h in range(heads):
            lanes = slice(h * HDIM, (h + 1) * HDIM)
            logits = scores[:, lanes] * (scaling * math.log2(math.e)) + bias
            peak = jnp.max(logits, axis=0, keepdims=True)
            powers = jnp.exp2(logits - peak)
            total = jnp.sum(powers, axis=0, keepdims=True)
            lse_ref[h : h + 1, pl.ds(pl.multiple_of(base, ROWS), ROWS)] = (
                peak * math.log(2.0) + jnp.log(total)
            )
            weights = powers * (1.0 / total)
            low = weights.astype(jnp.bfloat16)
            upper = grad_weights[:, lanes]
            delta = jnp.sum(low.astype(jnp.float32) * upper, axis=0, keepdims=True)
            weights_all.append(low)
            grad_all.append((weights * (upper - delta) * scaling).astype(jnp.bfloat16))
        weights_low = jnp.concatenate(weights_all, axis=1)
        grad_low = jnp.concatenate(grad_all, axis=1)
        dv_acc[window, :] += jnp.dot(weights_low, grads, preferred_element_type=jnp.float32)
        dk_acc[window, :] += jnp.dot(grad_low, queries, preferred_element_type=jnp.float32)
        dq_t = jnp.dot(kn_t_ref[:, window], grad_low, preferred_element_type=jnp.float32)
        inner = jnp.zeros((ROWS, HDIM), jnp.float32)
        for h in range(heads):
            lanes = slice(h * HDIM, (h + 1) * HDIM)
            low = jnp.transpose(dq_t[:, lanes]).astype(jnp.bfloat16)
            dq_ref[:, lanes] = low
            inner += low.astype(jnp.float32) * q_gain_ref[:, lanes] * q_ref[:, lanes].astype(
                jnp.float32
            )
        back_ref[pl.ds(step, 1), :] = row_sums(inner)

    for count in range(1, REACH // ROWS + 2):
        pl.when(needed == count)(functools.partial(block, count))

    @pl.when(step == blocks - 1)
    def _():
        dv_ref[...] = dv_acc[...].astype(jnp.bfloat16)
        for b in range(blocks):
            at = slice(b * ROWS, (b + 1) * ROWS)
            low = dk_acc[at, :].astype(jnp.bfloat16)
            dk_ref[at, :] = low
            back_ref[blocks + b : blocks + b + 1, :] = row_sums(
                low.astype(jnp.float32) * k_gain_ref[...] * k_ref[at, :].astype(jnp.float32)
            )
        slots_ref[...] = jnp.zeros_like(slots_ref)
        logs = lse_ref[...]
        home = jnp.zeros((8, home_count), jnp.float32)
        kept = jnp.int32(0)
        begin = jnp.int32(0)
        home_at = lax.broadcasted_iota(jnp.int32, (8, home_count), 1)
        for j in range(docs):
            length = len_ref[0, j]
            dest = dest_ref[0, j]
            stays = dest == here
            shift = jnp.where(stays, kept, off_ref[0, j])
            turned = pltpu.roll(logs, lax.rem(shift - begin + seq_len, seq_len), 1)
            inside = (home_at >= shift) & (home_at < shift + length)
            piece = jnp.where(inside, turned[:, :home_count], 0.0)
            home += jnp.where(stays, piece, 0.0)

            @pl.when(jnp.logical_not(stays))
            def _():
                slots_ref[dest] = piece[:, :slot]

            kept = kept + jnp.where(stays, length, 0)
            begin = begin + length
        home_ref[...] = home


def attention(q, k, v, d_out, recip_q, recip_k, q_gain, k_gain, lengths, dest, offset, devices, slot):
    seq_len, width = q.shape
    blocks = seq_len // ROWS
    home_count = seq_len // 4
    smem = pl.BlockSpec(memory_space=pltpu.SMEM)

    def whole(shape):
        return pl.BlockSpec(shape, lambda i: (0,) * len(shape))

    rows = pl.BlockSpec((ROWS, width), lambda i: (i, 0))
    kv = whole((seq_len, HDIM))
    return pl.pallas_call(
        functools.partial(attention_kernel, lengths.shape[1], devices, slot, home_count),
        grid=(blocks,),
        in_specs=[
            smem,
            smem,
            smem,
            rows,
            rows,
            kv,
            kv,
            whole((blocks, ROWS)),
            whole((blocks, ROWS)),
            whole((1, width)),
            whole((1, HDIM)),
        ],
        out_specs=[
            rows,
            kv,
            kv,
            whole((2 * blocks, ROWS)),
            whole((8, home_count)),
            whole((devices, 8, slot)),
        ],
        out_shape=[
            jax.ShapeDtypeStruct((seq_len, width), jnp.bfloat16),
            jax.ShapeDtypeStruct((seq_len, HDIM), jnp.bfloat16),
            jax.ShapeDtypeStruct((seq_len, HDIM), jnp.bfloat16),
            jax.ShapeDtypeStruct((2 * blocks, ROWS), jnp.float32),
            jax.ShapeDtypeStruct((8, home_count), jnp.float32),
            jax.ShapeDtypeStruct((devices, 8, slot), jnp.float32),
        ],
        scratch_shapes=[
            pltpu.VMEM((seq_len, HDIM), jnp.bfloat16),
            pltpu.VMEM((HDIM, seq_len), jnp.bfloat16),
            pltpu.VMEM((seq_len, HDIM), jnp.float32),
            pltpu.VMEM((seq_len, HDIM), jnp.float32),
            pltpu.VMEM((8, seq_len), jnp.float32),
        ],
        compiler_params=pltpu.CompilerParams(
            vmem_limit_bytes=48 * 1024 * 1024, dimension_semantics=("arbitrary",)
        ),
        cost_estimate=pl.CostEstimate(
            flops=10 * seq_len * REACH * width,
            bytes_accessed=8 * seq_len * width,
            transcendentals=seq_len * REACH * width // HDIM,
        ),
    )(lengths, dest, offset, q, d_out, k, v, recip_q, recip_k, q_gain, k_gain)


def local(q_raw, k_raw, v_proj, d_out, q_gain, k_gain, doc_lengths, plan_dest, plan_offset):
    seq_len = q_raw.shape[0]
    heads = q_raw.shape[1] // HDIM
    blocks = seq_len // ROWS
    devices = lax.axis_size("dp")
    span = 2 * seq_len
    slot = span // devices
    width_q = q_raw.shape[1] * lax.axis_size("head")
    width_k = k_raw.shape[1] * lax.axis_size("head")
    q_float = q_raw.astype(jnp.float32)
    k_float = k_raw.astype(jnp.float32)
    sums = lax.psum(
        jnp.stack([jnp.sum(q_float * q_float, axis=1), jnp.sum(k_float * k_float, axis=1)]), "head"
    )
    recip_q = lax.rsqrt(sums[0] / width_q + eps)
    recip_k = lax.rsqrt(sums[1] / width_k + eps)
    dq_norm, dk_norm, grad_v, back, home_log, slots = attention(
        q_raw,
        k_raw,
        v_proj,
        d_out,
        recip_q.reshape(blocks, ROWS),
        recip_k.reshape(blocks, ROWS),
        q_gain.reshape(1, -1),
        k_gain.reshape(1, -1),
        doc_lengths,
        plan_dest,
        plan_offset,
        devices,
        slot,
    )
    got = lax.all_to_all(slots, "dp", split_axis=0, concat_axis=0, tiled=True)
    away_log = jnp.transpose(got[:, :heads, :], (1, 0, 2)).reshape(heads, span)
    balanced = jnp.concatenate([home_log[:heads], away_log], axis=1)
    back = lax.psum(back, "head").reshape(2, seq_len)
    cube_q = recip_q * recip_q * recip_q * back[0] / width_q
    cube_k = recip_k * recip_k * recip_k * back[1] / width_k
    scaled_q = dq_norm.astype(jnp.float32) * q_gain[None, :]
    scaled_k = dk_norm.astype(jnp.float32) * k_gain[None, :]
    grad_q = (recip_q[:, None] * scaled_q - q_float * cube_q[:, None]).astype(jnp.bfloat16)
    grad_k = (recip_k[:, None] * scaled_k - k_float * cube_k[:, None]).astype(jnp.bfloat16)
    return (grad_q, grad_k, grad_v, balanced)


def solution(mesh):
    in_specs = (
        P("dp", "head"),
        P("dp", "head"),
        P("dp", "head"),
        P("dp", "head"),
        P("head"),
        P("head"),
        P("dp", None),
        P("dp", None),
        P("dp", None),
    )
    out_specs = (P("dp", "head"), P("dp", "head"), P("dp", "head"), P("head", "dp"))
    return jax.shard_map(local, mesh=mesh, in_specs=in_specs, out_specs=out_specs, check_vma=False)
```

```python
import functools
import math

import jax
import jax.numpy as jnp
from jax import lax
from jax.experimental import pallas as pl
from jax.experimental.pallas import tpu as pltpu
from jax.sharding import PartitionSpec as P

HDIM = 128
ROWS = 128
REACH = 384

eps = 1e-06
big_negative = -1e30


def column(row):
    return jnp.transpose(jnp.broadcast_to(row, (ROWS, ROWS)))


def row_sums(tile):
    return jnp.sum(jnp.transpose(tile), axis=0, keepdims=True)


def nt_dot(a, b):
    return lax.dot_general(a, b, (((1,), (1,)), ((), ())), preferred_element_type=jnp.float32)


def attention_kernel(
    docs,
    devices,
    slot,
    home_count,
    len_ref,
    dest_ref,
    off_ref,
    q_ref,
    grad_ref,
    k_ref,
    v_ref,
    recip_q_ref,
    recip_k_ref,
    q_gain_ref,
    k_gain_ref,
    dq_ref,
    dk_ref,
    dv_ref,
    back_ref,
    home_ref,
    slots_ref,
    kn_ref,
    kn_t_ref,
    dk_acc,
    dv_acc,
    lse_ref,
):
    step = pl.program_id(0)
    seq_len = k_ref.shape[0]
    blocks = seq_len // ROWS
    heads = q_ref.shape[1] // HDIM
    scaling = 1.0 / math.sqrt(HDIM)
    here = lax.axis_index("dp")

    @pl.when(step == 0)
    def _():
        dk_acc[...] = jnp.zeros_like(dk_acc)
        dv_acc[...] = jnp.zeros_like(dv_acc)
        lse_ref[...] = jnp.zeros_like(lse_ref)
        for b in range(blocks):
            at = slice(b * ROWS, (b + 1) * ROWS)
            normed = (
                k_ref[at, :].astype(jnp.float32)
                * column(recip_k_ref[b : b + 1, :])
                * k_gain_ref[...]
            )
            low = normed.astype(jnp.bfloat16)
            kn_ref[at, :] = low
            kn_t_ref[:, at] = jnp.transpose(low.astype(jnp.float32)).astype(jnp.bfloat16)

    base = step * ROWS
    token = base + lax.broadcasted_iota(jnp.int32, (1, ROWS), 1)
    start = jnp.zeros((1, ROWS), jnp.int32)
    first = jnp.int32(0)
    end = jnp.int32(0)
    for j in range(docs):
        end = end + len_ref[0, j]
        start = jnp.where(token >= end, end, start)
        first = jnp.where(base >= end, end, first)
    needed = step - first // ROWS + 1

    def block(count):
        width = count * ROWS
        key_at = pl.multiple_of((step - (count - 1)) * ROWS, ROWS)
        window = pl.ds(key_at, width)
        recip = column(recip_q_ref[pl.ds(step, 1), :])
        normed, upstream = [], []
        for h in range(heads):
            lanes = slice(h * HDIM, (h + 1) * HDIM)
            tile = q_ref[:, lanes].astype(jnp.float32) * recip * q_gain_ref[:, lanes]
            normed.append(tile.astype(jnp.bfloat16))
            upstream.append(grad_ref[:, lanes])
        queries = jnp.concatenate(normed, axis=0)
        grads = jnp.concatenate(upstream, axis=0)
        scores = nt_dot(kn_ref[window, :], queries)
        grad_weights = nt_dot(v_ref[window, :], grads)
        key = key_at + lax.broadcasted_iota(jnp.int32, (width, ROWS), 0)
        bias = jnp.where((key >= start) & (key <= token), 0.0, big_negative)
        weights_all, grad_all = [], []
        for h in range(heads):
            lanes = slice(h * HDIM, (h + 1) * HDIM)
            logits = scores[:, lanes] * (scaling * math.log2(math.e)) + bias
            peak = jnp.max(logits, axis=0, keepdims=True)
            powers = jnp.exp2(logits - peak)
            total = jnp.sum(powers, axis=0, keepdims=True)
            lse_ref[h : h + 1, pl.ds(pl.multiple_of(base, ROWS), ROWS)] = (
                peak * math.log(2.0) + jnp.log(total)
            )
            weights = powers * (1.0 / total)
            low = weights.astype(jnp.bfloat16)
            upper = grad_weights[:, lanes]
            delta = jnp.sum(low.astype(jnp.float32) * upper, axis=0, keepdims=True)
            weights_all.append(low)
            grad_all.append((weights * (upper - delta) * scaling).astype(jnp.bfloat16))
        weights_low = jnp.concatenate(weights_all, axis=1)
        grad_low = jnp.concatenate(grad_all, axis=1)
        dv_acc[window, :] += jnp.dot(weights_low, grads, preferred_element_type=jnp.float32)
        dk_acc[window, :] += jnp.dot(grad_low, queries, preferred_element_type=jnp.float32)
        dq_t = jnp.dot(kn_t_ref[:, window], grad_low, preferred_element_type=jnp.float32)
        inner = jnp.zeros((ROWS, HDIM), jnp.float32)
        for h in range(heads):
            lanes = slice(h * HDIM, (h + 1) * HDIM)
            low = jnp.transpose(dq_t[:, lanes]).astype(jnp.bfloat16)
            dq_ref[:, lanes] = low
            inner += low.astype(jnp.float32) * q_gain_ref[:, lanes] * q_ref[:, lanes].astype(
                jnp.float32
            )
        back_ref[pl.ds(step, 1), :] = row_sums(inner)

    for count in range(1, REACH // ROWS + 2):
        pl.when(needed == count)(functools.partial(block, count))

    @pl.when(step == blocks - 1)
    def _():
        dv_ref[...] = dv_acc[...].astype(jnp.bfloat16)
        for b in range(blocks):
            at = slice(b * ROWS, (b + 1) * ROWS)
            low = dk_acc[at, :].astype(jnp.bfloat16)
            dk_ref[at, :] = low
            back_ref[blocks + b : blocks + b + 1, :] = row_sums(
                low.astype(jnp.float32) * k_gain_ref[...] * k_ref[at, :].astype(jnp.float32)
            )
        slots_ref[...] = jnp.zeros_like(slots_ref)
        logs = lse_ref[...]
        home = jnp.zeros((8, home_count), jnp.float32)
        kept = jnp.int32(0)
        begin = jnp.int32(0)
        home_at = lax.broadcasted_iota(jnp.int32, (8, home_count), 1)
        for j in range(docs):
            length = len_ref[0, j]
            dest = dest_ref[0, j]
            stays = dest == here
            shift = jnp.where(stays, kept, off_ref[0, j])
            turned = pltpu.roll(logs, lax.rem(shift - begin + seq_len, seq_len), 1)
            inside = (home_at >= shift) & (home_at < shift + length)
            piece = jnp.where(inside, turned[:, :home_count], 0.0)
            home += jnp.where(stays, piece, 0.0)

            @pl.when(jnp.logical_not(stays))
            def _():
                slots_ref[dest] = piece[:, :slot]

            kept = kept + jnp.where(stays, length, 0)
            begin = begin + length
        home_ref[...] = home


def attention(q, k, v, d_out, recip_q, recip_k, q_gain, k_gain, lengths, dest, offset, devices, slot):
    seq_len, width = q.shape
    blocks = seq_len // ROWS
    home_count = seq_len // 4
    smem = pl.BlockSpec(memory_space=pltpu.SMEM)

    def whole(shape):
        return pl.BlockSpec(shape, lambda i: (0,) * len(shape))

    rows = pl.BlockSpec((ROWS, width), lambda i: (i, 0))
    kv = whole((seq_len, HDIM))
    return pl.pallas_call(
        functools.partial(attention_kernel, lengths.shape[1], devices, slot, home_count),
        grid=(blocks,),
        in_specs=[
            smem,
            smem,
            smem,
            rows,
            rows,
            kv,
            kv,
            whole((blocks, ROWS)),
            whole((blocks, ROWS)),
            whole((1, width)),
            whole((1, HDIM)),
        ],
        out_specs=[
            rows,
            kv,
            kv,
            whole((2 * blocks, ROWS)),
            whole((8, home_count)),
            whole((devices, 8, slot)),
        ],
        out_shape=[
            jax.ShapeDtypeStruct((seq_len, width), jnp.bfloat16),
            jax.ShapeDtypeStruct((seq_len, HDIM), jnp.bfloat16),
            jax.ShapeDtypeStruct((seq_len, HDIM), jnp.bfloat16),
            jax.ShapeDtypeStruct((2 * blocks, ROWS), jnp.float32),
            jax.ShapeDtypeStruct((8, home_count), jnp.float32),
            jax.ShapeDtypeStruct((devices, 8, slot), jnp.float32),
        ],
        scratch_shapes=[
            pltpu.VMEM((seq_len, HDIM), jnp.bfloat16),
            pltpu.VMEM((HDIM, seq_len), jnp.bfloat16),
            pltpu.VMEM((seq_len, HDIM), jnp.float32),
            pltpu.VMEM((seq_len, HDIM), jnp.float32),
            pltpu.VMEM((8, seq_len), jnp.float32),
        ],
        compiler_params=pltpu.CompilerParams(
            vmem_limit_bytes=48 * 1024 * 1024, dimension_semantics=("arbitrary",)
        ),
        cost_estimate=pl.CostEstimate(
            flops=10 * seq_len * REACH * width,
            bytes_accessed=8 * seq_len * width,
            transcendentals=seq_len * REACH * width // HDIM,
        ),
    )(lengths, dest, offset, q, d_out, k, v, recip_q, recip_k, q_gain, k_gain)


def peer_sum(parts_ref, got_ref, send_sem, recv_sem, me, peers):
    copies = []
    for d in range(1, peers):
        copy = pltpu.make_async_remote_copy(
            src_ref=parts_ref,
            dst_ref=got_ref.at[d - 1],
            send_sem=send_sem.at[d - 1],
            recv_sem=recv_sem.at[d - 1],
            device_id={"head": lax.rem(me + d, peers)},
            device_id_type=pl.DeviceIdType.MESH,
        )
        copy.start()
        copies.append(copy)
    return copies


def stat_kernel(peers, q_ref, k_ref, recip_ref, parts_ref, got_ref, send_sem, recv_sem):
    me = lax.axis_index("head")
    seq_len, width = q_ref.shape
    blocks = seq_len // ROWS
    barrier = pltpu.get_barrier_semaphore()
    for d in range(1, peers):
        pl.semaphore_signal(
            barrier,
            inc=1,
            device_id={"head": lax.rem(me + d, peers)},
            device_id_type=pl.DeviceIdType.MESH,
        )
    for b in range(blocks):
        at = slice(b * ROWS, (b + 1) * ROWS)
        total = jnp.zeros((ROWS, HDIM), jnp.float32)
        for h in range(width // HDIM):
            tile = q_ref[at, h * HDIM : (h + 1) * HDIM].astype(jnp.float32)
            total += tile * tile
        parts_ref[b : b + 1, :] = row_sums(total)
        tile = k_ref[at, :].astype(jnp.float32)
        parts_ref[blocks + b : blocks + b + 1, :] = row_sums(tile * tile)
    pl.semaphore_wait(barrier, peers - 1)
    copies = peer_sum(parts_ref, got_ref, send_sem, recv_sem, me, peers)
    for copy in copies:
        copy.wait()
    sums = parts_ref[...]
    for d in range(peers - 1):
        sums += got_ref[d]
    recip_ref[:blocks, :] = lax.rsqrt(sums[:blocks] / (width * peers) + eps)
    recip_ref[blocks:, :] = lax.rsqrt(sums[blocks:] / (HDIM * peers) + eps)


def token_scales(q, k, peers):
    blocks = q.shape[0] // ROWS
    vmem = pl.BlockSpec(memory_space=pltpu.VMEM)
    return pl.pallas_call(
        functools.partial(stat_kernel, peers),
        out_shape=jax.ShapeDtypeStruct((2 * blocks, ROWS), jnp.float32),
        in_specs=[vmem, vmem],
        out_specs=vmem,
        scratch_shapes=[
            pltpu.VMEM((2 * blocks, ROWS), jnp.float32),
            pltpu.VMEM((peers - 1, 2 * blocks, ROWS), jnp.float32),
            pltpu.SemaphoreType.DMA((peers - 1,)),
            pltpu.SemaphoreType.DMA((peers - 1,)),
        ],
        compiler_params=pltpu.CompilerParams(
            collective_id=0, has_side_effects=True, vmem_limit_bytes=32 * 1024 * 1024
        ),
    )(q, k)


def finish_kernel(
    peers,
    devices,
    width_q,
    recip_ref,
    back_ref,
    slots_ref,
    cube_ref,
    logs_ref,
    got_ref,
    log_got_ref,
    send_sem,
    recv_sem,
    log_send_sem,
    log_recv_sem,
):
    me = lax.axis_index("head")
    here = lax.axis_index("dp")
    rows = back_ref.shape[0]
    blocks = rows // 2
    barrier = pltpu.get_barrier_semaphore()
    for d in range(1, peers):
        pl.semaphore_signal(
            barrier,
            inc=1,
            device_id={"head": lax.rem(me + d, peers)},
            device_id_type=pl.DeviceIdType.MESH,
        )
    for d in range(1, devices):
        pl.semaphore_signal(
            barrier,
            inc=1,
            device_id={"dp": lax.rem(here + d, devices)},
            device_id_type=pl.DeviceIdType.MESH,
        )
    pl.semaphore_wait(barrier, peers - 1 + devices - 1)
    copies = peer_sum(back_ref, got_ref, send_sem, recv_sem, me, peers)
    log_copies = []
    for d in range(1, devices):
        there = lax.rem(here + d, devices)
        copy = pltpu.make_async_remote_copy(
            src_ref=slots_ref.at[there],
            dst_ref=log_got_ref.at[here],
            send_sem=log_send_sem.at[d - 1],
            recv_sem=log_recv_sem.at[d - 1],
            device_id={"dp": there},
            device_id_type=pl.DeviceIdType.MESH,
        )
        copy.start()
        log_copies.append(copy)
    for copy in copies:
        copy.wait()
    sums = back_ref[...]
    for d in range(peers - 1):
        sums += got_ref[d]
    recip = recip_ref[...]
    cubes = recip * recip * recip * sums
    cube_ref[:blocks, :] = cubes[:blocks] / width_q
    cube_ref[blocks:, :] = cubes[blocks:] / (HDIM * peers)
    for copy in log_copies:
        copy.wait()
    log_got_ref[here] = jnp.zeros(log_got_ref.shape[1:], jnp.float32)
    logs_ref[...] = log_got_ref[...]


def finish(recip, back, slots, peers, width):
    devices, pad, slot = slots.shape
    vmem = pl.BlockSpec(memory_space=pltpu.VMEM)
    return pl.pallas_call(
        functools.partial(finish_kernel, peers, devices, width * peers),
        out_shape=[
            jax.ShapeDtypeStruct(back.shape, jnp.float32),
            jax.ShapeDtypeStruct(slots.shape, jnp.float32),
        ],
        in_specs=[vmem, vmem, vmem],
        out_specs=[vmem, vmem],
        scratch_shapes=[
            pltpu.VMEM((peers - 1,) + back.shape, jnp.float32),
            pltpu.VMEM(slots.shape, jnp.float32),
            pltpu.SemaphoreType.DMA((peers - 1,)),
            pltpu.SemaphoreType.DMA((peers - 1,)),
            pltpu.SemaphoreType.DMA((devices - 1,)),
            pltpu.SemaphoreType.DMA((devices - 1,)),
        ],
        compiler_params=pltpu.CompilerParams(
            collective_id=1, has_side_effects=True, vmem_limit_bytes=32 * 1024 * 1024
        ),
    )(recip, back, slots)


def local(q_raw, k_raw, v_proj, d_out, q_gain, k_gain, doc_lengths, plan_dest, plan_offset):
    seq_len = q_raw.shape[0]
    heads = q_raw.shape[1] // HDIM
    blocks = seq_len // ROWS
    devices = lax.axis_size("dp")
    peers = lax.axis_size("head")
    span = 2 * seq_len
    slot = span // devices
    recip = token_scales(q_raw, k_raw, peers)
    dq_norm, dk_norm, grad_v, back, home_log, slots = attention(
        q_raw,
        k_raw,
        v_proj,
        d_out,
        recip[:blocks],
        recip[blocks:],
        q_gain.reshape(1, -1),
        k_gain.reshape(1, -1),
        doc_lengths,
        plan_dest,
        plan_offset,
        devices,
        slot,
    )
    cubes, got = finish(recip, back, slots, peers, q_raw.shape[1])
    away_log = jnp.transpose(got[:, :heads, :], (1, 0, 2)).reshape(heads, span)
    balanced = jnp.concatenate([home_log[:heads], away_log], axis=1)
    recip = recip.reshape(2, seq_len)
    cubes = cubes.reshape(2, seq_len)
    scaled_q = dq_norm.astype(jnp.float32) * q_gain[None, :]
    scaled_k = dk_norm.astype(jnp.float32) * k_gain[None, :]
    q_float = q_raw.astype(jnp.float32)
    k_float = k_raw.astype(jnp.float32)
    grad_q = (recip[0][:, None] * scaled_q - q_float * cubes[0][:, None]).astype(jnp.bfloat16)
    grad_k = (recip[1][:, None] * scaled_k - k_float * cubes[1][:, None]).astype(jnp.bfloat16)
    return (grad_q, grad_k, grad_v, balanced)


def solution(mesh):
    in_specs = (
        P("dp", "head"),
        P("dp", "head"),
        P("dp", "head"),
        P("dp", "head"),
        P("head"),
        P("head"),
        P("dp", None),
        P("dp", None),
        P("dp", None),
    )
    out_specs = (P("dp", "head"), P("dp", "head"), P("dp", "head"), P("head", "dp"))
    return jax.shard_map(local, mesh=mesh, in_specs=in_specs, out_specs=out_specs, check_vma=False)
```

```python
import functools
import math

import jax
import jax.numpy as jnp
from jax import lax
from jax.experimental import pallas as pl
from jax.experimental.pallas import tpu as pltpu
from jax.sharding import PartitionSpec as P

HDIM = 128
ROWS = 128
REACH = 384
CHUNKS = 4
STEP_BLOCKS = 3

eps = 1e-06
big_negative = -1e30


def column(row):
    return jnp.transpose(jnp.broadcast_to(row, (ROWS, ROWS)))


def row_sums(tile):
    return jnp.sum(jnp.transpose(tile), axis=0, keepdims=True)


def nt_dot(a, b):
    return lax.dot_general(a, b, (((1,), (1,)), ((), ())), preferred_element_type=jnp.float32)


def attention_kernel(
    docs,
    devices,
    slot,
    home_count,
    len_ref,
    dest_ref,
    off_ref,
    q_ref,
    grad_ref,
    k_ref,
    v_ref,
    recip_ref,
    q_gain_ref,
    k_gain_ref,
    dq_ref,
    dk_ref,
    dv_ref,
    back_ref,
    home_ref,
    slots_ref,
    kn_ref,
    kn_t_ref,
    dk_acc,
    dv_acc,
    lse_ref,
):
    step = pl.program_id(0)
    seq_len = k_ref.shape[0]
    blocks = seq_len // ROWS
    heads = q_ref.shape[1] // HDIM
    scaling = 1.0 / math.sqrt(HDIM)
    here = lax.axis_index("dp")

    @pl.when(step == 0)
    def _():
        dk_acc[...] = jnp.zeros_like(dk_acc)
        dv_acc[...] = jnp.zeros_like(dv_acc)
        lse_ref[...] = jnp.zeros_like(lse_ref)
        for b in range(blocks):
            at = slice(b * ROWS, (b + 1) * ROWS)
            normed = (
                k_ref[at, :].astype(jnp.float32)
                * column(recip_ref[blocks + b : blocks + b + 1, :])
                * k_gain_ref[...]
            )
            low = normed.astype(jnp.bfloat16)
            kn_ref[at, :] = low
            kn_t_ref[:, at] = jnp.transpose(low.astype(jnp.float32)).astype(jnp.bfloat16)

    def block(index, start, token, count):
        width = count * ROWS
        key_at = pl.multiple_of((index - (count - 1)) * ROWS, ROWS)
        window = pl.ds(key_at, width)
        here_at = pl.multiple_of(index * ROWS, ROWS)
        mine = pl.ds(pl.multiple_of(lax.rem(index, STEP_BLOCKS) * ROWS, ROWS), ROWS)
        recip = column(recip_ref[pl.ds(index, 1), :])
        key = key_at + lax.broadcasted_iota(jnp.int32, (width, ROWS), 0)
        bias = jnp.where((key >= start) & (key <= token), 0.0, big_negative)
        keys = kn_ref[window, :]
        values = v_ref[window, :]
        keys_t = kn_t_ref[:, window]

        def products(group):
            normed, upstream = [], []
            for h in group:
                lanes = slice(h * HDIM, (h + 1) * HDIM)
                tile = q_ref[mine, lanes].astype(jnp.float32) * recip * q_gain_ref[:, lanes]
                normed.append(tile.astype(jnp.bfloat16))
                upstream.append(grad_ref[mine, lanes])
            queries = jnp.concatenate(normed, axis=0)
            grads = jnp.concatenate(upstream, axis=0)
            return queries, grads, nt_dot(keys, queries), nt_dot(values, grads)

        def softmax(group, scores, grad_weights):
            weights_all, grad_all = [], []
            for n, h in enumerate(group):
                lanes = slice(n * HDIM, (n + 1) * HDIM)
                logits = scores[:, lanes] * (scaling * math.log2(math.e)) + bias
                peak = jnp.max(logits, axis=0, keepdims=True)
                powers = jnp.exp2(logits - peak)
                total = jnp.sum(powers, axis=0, keepdims=True)
                lse_ref[h : h + 1, pl.ds(here_at, ROWS)] = peak * math.log(2.0) + jnp.log(total)
                weights = powers * (1.0 / total)
                low = weights.astype(jnp.bfloat16)
                upper = grad_weights[:, lanes]
                delta = jnp.sum(low.astype(jnp.float32) * upper, axis=0, keepdims=True)
                weights_all.append(low)
                grad_all.append((weights * (upper - delta) * scaling).astype(jnp.bfloat16))
            return jnp.concatenate(weights_all, axis=1), jnp.concatenate(grad_all, axis=1)

        def gradients(group, queries, grads, weights_low, grad_low):
            dv = jnp.dot(weights_low, grads, preferred_element_type=jnp.float32)
            dk = jnp.dot(grad_low, queries, preferred_element_type=jnp.float32)
            dq_t = jnp.dot(keys_t, grad_low, preferred_element_type=jnp.float32)
            inner = jnp.zeros((ROWS, HDIM), jnp.float32)
            for n, h in enumerate(group):
                lanes = slice(h * HDIM, (h + 1) * HDIM)
                low = jnp.transpose(dq_t[:, n * HDIM : (n + 1) * HDIM]).astype(jnp.bfloat16)
                dq_ref[mine, lanes] = low
                inner += (
                    low.astype(jnp.float32)
                    * q_gain_ref[:, lanes]
                    * q_ref[mine, lanes].astype(jnp.float32)
                )
            return dv, dk, inner

        groups = [range(h, min(h + 2, heads)) for h in range(0, heads, 2)]
        ready = [products(groups[0])]
        results = []
        for n, group in enumerate(groups):
            if n + 1 < len(groups):
                ready.append(products(groups[n + 1]))
            queries, grads, scores, grad_weights = ready[n]
            weights_low, grad_low = softmax(group, scores, grad_weights)
            results.append(gradients(group, queries, grads, weights_low, grad_low))
        dv_acc[window, :] += sum(r[0] for r in results)
        dk_acc[window, :] += sum(r[1] for r in results)
        back_ref[pl.ds(index, 1), :] = row_sums(sum(r[2] for r in results))

    @pl.loop(0, STEP_BLOCKS)
    def _(part):
        index = step * STEP_BLOCKS + part
        base = index * ROWS
        token = base + lax.broadcasted_iota(jnp.int32, (1, ROWS), 1)
        start = jnp.zeros((1, ROWS), jnp.int32)
        first = jnp.int32(0)
        end = jnp.int32(0)
        for j in range(docs):
            end = end + len_ref[0, j]
            start = jnp.where(token >= end, end, start)
            first = jnp.where(base >= end, end, first)
        needed = index - first // ROWS + 1
        for count in range(1, REACH // ROWS + 2):
            pl.when(needed == count)(functools.partial(block, index, start, token, count))

    @pl.when(step == pl.num_programs(0) - 1)
    def _():
        dv_ref[...] = dv_acc[...].astype(jnp.bfloat16)
        for b in range(blocks):
            at = slice(b * ROWS, (b + 1) * ROWS)
            low = dk_acc[at, :].astype(jnp.bfloat16)
            dk_ref[at, :] = low
            back_ref[blocks + b : blocks + b + 1, :] = row_sums(
                low.astype(jnp.float32) * k_gain_ref[...] * k_ref[at, :].astype(jnp.float32)
            )
        slots_ref[...] = jnp.zeros_like(slots_ref)
        logs = lse_ref[...]
        home = jnp.zeros((8, home_count), jnp.float32)
        kept = jnp.int32(0)
        begin = jnp.int32(0)
        home_at = lax.broadcasted_iota(jnp.int32, (8, home_count), 1)
        for j in range(docs):
            length = len_ref[0, j]
            dest = dest_ref[0, j]
            stays = dest == here
            shift = jnp.where(stays, kept, off_ref[0, j])
            turned = pltpu.roll(logs, lax.rem(shift - begin + seq_len, seq_len), 1)
            inside = (home_at >= shift) & (home_at < shift + length)
            piece = jnp.where(inside, turned[:, :home_count], 0.0)
            home += jnp.where(stays, piece, 0.0)

            @pl.when(jnp.logical_not(stays))
            def _():
                slots_ref[dest] = piece[:, :slot]

            kept = kept + jnp.where(stays, length, 0)
            begin = begin + length
        home_ref[...] = home


def attention(q, k, v, d_out, recip, q_gain, k_gain, lengths, dest, offset, devices, slot):
    seq_len, width = q.shape
    blocks = seq_len // ROWS
    home_count = seq_len // 4
    smem = pl.BlockSpec(memory_space=pltpu.SMEM)

    def whole(shape):
        return pl.BlockSpec(shape, lambda i: (0,) * len(shape))

    rows = pl.BlockSpec((ROWS * STEP_BLOCKS, width), lambda i: (i, 0))
    kv = whole((seq_len, HDIM))
    return pl.pallas_call(
        functools.partial(attention_kernel, lengths.shape[1], devices, slot, home_count),
        grid=(blocks // STEP_BLOCKS,),
        in_specs=[
            smem,
            smem,
            smem,
            rows,
            rows,
            kv,
            kv,
            whole((2 * blocks, ROWS)),
            whole((1, width)),
            whole((1, HDIM)),
        ],
        out_specs=[
            rows,
            kv,
            kv,
            whole((2 * blocks, ROWS)),
            whole((8, home_count)),
            whole((devices, 8, slot)),
        ],
        out_shape=[
            jax.ShapeDtypeStruct((seq_len, width), jnp.bfloat16),
            jax.ShapeDtypeStruct((seq_len, HDIM), jnp.bfloat16),
            jax.ShapeDtypeStruct((seq_len, HDIM), jnp.bfloat16),
            jax.ShapeDtypeStruct((2 * blocks, ROWS), jnp.float32),
            jax.ShapeDtypeStruct((8, home_count), jnp.float32),
            jax.ShapeDtypeStruct((devices, 8, slot), jnp.float32),
        ],
        scratch_shapes=[
            pltpu.VMEM((seq_len, HDIM), jnp.bfloat16),
            pltpu.VMEM((HDIM, seq_len), jnp.bfloat16),
            pltpu.VMEM((seq_len, HDIM), jnp.float32),
            pltpu.VMEM((seq_len, HDIM), jnp.float32),
            pltpu.VMEM((8, seq_len), jnp.float32),
        ],
        compiler_params=pltpu.CompilerParams(
            vmem_limit_bytes=48 * 1024 * 1024, dimension_semantics=("arbitrary",)
        ),
        cost_estimate=pl.CostEstimate(
            flops=10 * seq_len * REACH * width,
            bytes_accessed=8 * seq_len * width,
            transcendentals=seq_len * REACH * width // HDIM,
        ),
    )(lengths, dest, offset, q, d_out, k, v, recip, q_gain, k_gain)


def peer_sum(parts_ref, got_ref, send_sem, recv_sem, me, peers):
    copies = []
    for d in range(1, peers):
        copy = pltpu.make_async_remote_copy(
            src_ref=parts_ref,
            dst_ref=got_ref.at[d - 1],
            send_sem=send_sem.at[d - 1],
            recv_sem=recv_sem.at[d - 1],
            device_id={"head": lax.rem(me + d, peers)},
            device_id_type=pl.DeviceIdType.MESH,
        )
        copy.start()
        copies.append(copy)
    return copies


def stat_kernel(
    peers, q_hbm, k_hbm, recip_ref, q_ref, k_ref, parts_ref, got_ref, send_sem, recv_sem, load_sem
):
    me = lax.axis_index("head")
    seq_len, width = q_ref.shape
    blocks = seq_len // ROWS
    part = seq_len // CHUNKS
    loads = [pltpu.make_async_copy(k_hbm, k_ref, load_sem.at[CHUNKS])]
    for c in range(CHUNKS):
        at = pl.ds(c * part, part)
        loads.append(pltpu.make_async_copy(q_hbm.at[at], q_ref.at[at], load_sem.at[c]))
    for load in loads:
        load.start()
    barrier = pltpu.get_barrier_semaphore()
    for d in range(1, peers):
        pl.semaphore_signal(
            barrier,
            inc=1,
            device_id={"head": lax.rem(me + d, peers)},
            device_id_type=pl.DeviceIdType.MESH,
        )
    loads[0].wait()
    for b in range(blocks):
        at = slice(b * ROWS, (b + 1) * ROWS)
        tile = k_ref[at, :].astype(jnp.float32)
        parts_ref[blocks + b : blocks + b + 1, :] = row_sums(tile * tile)
    for b in range(blocks):
        if b % (blocks // CHUNKS) == 0:
            loads[1 + b // (blocks // CHUNKS)].wait()
        at = slice(b * ROWS, (b + 1) * ROWS)
        total = jnp.zeros((ROWS, HDIM), jnp.float32)
        for h in range(width // HDIM):
            tile = q_ref[at, h * HDIM : (h + 1) * HDIM].astype(jnp.float32)
            total += tile * tile
        parts_ref[b : b + 1, :] = row_sums(total)
    pl.semaphore_wait(barrier, peers - 1)
    copies = peer_sum(parts_ref, got_ref, send_sem, recv_sem, me, peers)
    for copy in copies:
        copy.wait()
    sums = parts_ref[...]
    for d in range(peers - 1):
        sums += got_ref[d]
    recip_ref[:blocks, :] = lax.rsqrt(sums[:blocks] / (width * peers) + eps)
    recip_ref[blocks:, :] = lax.rsqrt(sums[blocks:] / (HDIM * peers) + eps)


def token_scales(q, k, peers):
    blocks = q.shape[0] // ROWS
    vmem = pl.BlockSpec(memory_space=pltpu.VMEM)
    return pl.pallas_call(
        functools.partial(stat_kernel, peers),
        out_shape=jax.ShapeDtypeStruct((2 * blocks, ROWS), jnp.float32),
        in_specs=[pl.BlockSpec(memory_space=pl.ANY)] * 2,
        out_specs=vmem,
        scratch_shapes=[
            pltpu.VMEM(q.shape, q.dtype),
            pltpu.VMEM(k.shape, k.dtype),
            pltpu.VMEM((2 * blocks, ROWS), jnp.float32),
            pltpu.VMEM((peers - 1, 2 * blocks, ROWS), jnp.float32),
            pltpu.SemaphoreType.DMA((peers - 1,)),
            pltpu.SemaphoreType.DMA((peers - 1,)),
            pltpu.SemaphoreType.DMA((CHUNKS + 1,)),
        ],
        compiler_params=pltpu.CompilerParams(
            collective_id=0, has_side_effects=True, vmem_limit_bytes=32 * 1024 * 1024
        ),
    )(q, k)


def finish_kernel(
    peers,
    devices,
    width_q,
    recip_ref,
    back_ref,
    slots_ref,
    cube_ref,
    logs_ref,
    got_ref,
    log_got_ref,
    send_sem,
    recv_sem,
    log_send_sem,
    log_recv_sem,
):
    me = lax.axis_index("head")
    here = lax.axis_index("dp")
    rows = back_ref.shape[0]
    blocks = rows // 2
    barrier = pltpu.get_barrier_semaphore()
    for d in range(1, peers):
        pl.semaphore_signal(
            barrier,
            inc=1,
            device_id={"head": lax.rem(me + d, peers)},
            device_id_type=pl.DeviceIdType.MESH,
        )
    for d in range(1, devices):
        pl.semaphore_signal(
            barrier,
            inc=1,
            device_id={"dp": lax.rem(here + d, devices)},
            device_id_type=pl.DeviceIdType.MESH,
        )
    pl.semaphore_wait(barrier, peers - 1 + devices - 1)
    copies = peer_sum(back_ref, got_ref, send_sem, recv_sem, me, peers)
    log_copies = []
    for d in range(1, devices):
        there = lax.rem(here + d, devices)
        copy = pltpu.make_async_remote_copy(
            src_ref=slots_ref.at[there],
            dst_ref=log_got_ref.at[here],
            send_sem=log_send_sem.at[d - 1],
            recv_sem=log_recv_sem.at[d - 1],
            device_id={"dp": there},
            device_id_type=pl.DeviceIdType.MESH,
        )
        copy.start()
        log_copies.append(copy)
    for copy in copies:
        copy.wait()
    sums = back_ref[...]
    for d in range(peers - 1):
        sums += got_ref[d]
    recip = recip_ref[...]
    cubes = recip * recip * recip * sums
    cube_ref[:blocks, :] = cubes[:blocks] / width_q
    cube_ref[blocks:, :] = cubes[blocks:] / (HDIM * peers)
    for copy in log_copies:
        copy.wait()
    log_got_ref[here] = jnp.zeros(log_got_ref.shape[1:], jnp.float32)
    logs_ref[...] = log_got_ref[...]


def finish(recip, back, slots, peers, width):
    devices, pad, slot = slots.shape
    vmem = pl.BlockSpec(memory_space=pltpu.VMEM)
    return pl.pallas_call(
        functools.partial(finish_kernel, peers, devices, width * peers),
        out_shape=[
            jax.ShapeDtypeStruct(back.shape, jnp.float32),
            jax.ShapeDtypeStruct(slots.shape, jnp.float32),
        ],
        in_specs=[vmem, vmem, vmem],
        out_specs=[vmem, vmem],
        scratch_shapes=[
            pltpu.VMEM((peers - 1,) + back.shape, jnp.float32),
            pltpu.VMEM(slots.shape, jnp.float32),
            pltpu.SemaphoreType.DMA((peers - 1,)),
            pltpu.SemaphoreType.DMA((peers - 1,)),
            pltpu.SemaphoreType.DMA((devices - 1,)),
            pltpu.SemaphoreType.DMA((devices - 1,)),
        ],
        compiler_params=pltpu.CompilerParams(
            collective_id=1, has_side_effects=True, vmem_limit_bytes=32 * 1024 * 1024
        ),
    )(recip, back, slots)


def local(q_raw, k_raw, v_proj, d_out, q_gain, k_gain, doc_lengths, plan_dest, plan_offset):
    seq_len = q_raw.shape[0]
    heads = q_raw.shape[1] // HDIM
    blocks = seq_len // ROWS
    devices = lax.axis_size("dp")
    peers = lax.axis_size("head")
    span = 2 * seq_len
    slot = span // devices
    recip = token_scales(q_raw, k_raw, peers)
    dq_norm, dk_norm, grad_v, back, home_log, slots = attention(
        q_raw,
        k_raw,
        v_proj,
        d_out,
        recip,
        q_gain.reshape(1, -1),
        k_gain.reshape(1, -1),
        doc_lengths,
        plan_dest,
        plan_offset,
        devices,
        slot,
    )
    cubes, got = finish(recip, back, slots, peers, q_raw.shape[1])
    away_log = jnp.transpose(got[:, :heads, :], (1, 0, 2)).reshape(heads, span)
    balanced = jnp.concatenate([home_log[:heads], away_log], axis=1)
    recip = recip.reshape(2, seq_len)
    cubes = cubes.reshape(2, seq_len)
    scaled_q = dq_norm.astype(jnp.float32) * q_gain[None, :]
    scaled_k = dk_norm.astype(jnp.float32) * k_gain[None, :]
    q_float = q_raw.astype(jnp.float32)
    k_float = k_raw.astype(jnp.float32)
    grad_q = (recip[0][:, None] * scaled_q - q_float * cubes[0][:, None]).astype(jnp.bfloat16)
    grad_k = (recip[1][:, None] * scaled_k - k_float * cubes[1][:, None]).astype(jnp.bfloat16)
    return (grad_q, grad_k, grad_v, balanced)


def solution(mesh):
    in_specs = (
        P("dp", "head"),
        P("dp", "head"),
        P("dp", "head"),
        P("dp", "head"),
        P("head"),
        P("head"),
        P("dp", None),
        P("dp", None),
        P("dp", None),
    )
    out_specs = (P("dp", "head"), P("dp", "head"), P("dp", "head"), P("head", "dp"))
    return jax.shard_map(local, mesh=mesh, in_specs=in_specs, out_specs=out_specs, check_vma=False)
```

```python
import functools
import math

import jax
import jax.numpy as jnp
from jax import lax
from jax.experimental import pallas as pl
from jax.experimental.pallas import tpu as pltpu
from jax.sharding import PartitionSpec as P

HDIM = 128
ROWS = 128
REACH = 384
CHUNKS = 4
TILE = 2

eps = 1e-06
big_negative = -1e30


def column(row):
    return jnp.transpose(jnp.broadcast_to(row, (ROWS, ROWS)))


def row_sums(tile):
    return jnp.sum(jnp.transpose(tile), axis=0, keepdims=True)


def nt_dot(a, b):
    return lax.dot_general(a, b, (((1,), (1,)), ((), ())), preferred_element_type=jnp.float32)


def attention_kernel(
    docs,
    devices,
    slot,
    home_count,
    len_ref,
    dest_ref,
    off_ref,
    q_ref,
    grad_ref,
    k_ref,
    v_hbm,
    recip_ref,
    q_gain_ref,
    k_gain_ref,
    dq_ref,
    dk_ref,
    dv_ref,
    back_ref,
    home_ref,
    slots_ref,
    kn_ref,
    kn_t_ref,
    dk_acc,
    dv_acc,
    lse_ref,
    v_ref,
    v_sem,
):
    step = pl.program_id(0)
    seq_len = k_ref.shape[0]
    blocks = seq_len // ROWS
    heads = q_ref.shape[1] // HDIM
    scaling = 1.0 / math.sqrt(HDIM)
    here = lax.axis_index("dp")

    @pl.when(step == 0)
    def _():
        load = pltpu.make_async_copy(v_hbm, v_ref, v_sem)
        load.start()
        dk_acc[...] = jnp.zeros_like(dk_acc)
        dv_acc[...] = jnp.zeros_like(dv_acc)
        lse_ref[...] = jnp.zeros_like(lse_ref)
        for b in range(blocks):
            at = slice(b * ROWS, (b + 1) * ROWS)
            normed = (
                k_ref[at, :].astype(jnp.float32)
                * column(recip_ref[blocks + b : blocks + b + 1, :])
                * k_gain_ref[...]
            )
            low = normed.astype(jnp.bfloat16)
            kn_ref[at, :] = low
            kn_t_ref[:, at] = jnp.transpose(low.astype(jnp.float32)).astype(jnp.bfloat16)
        load.wait()

    base = step * TILE * ROWS
    token = base + lax.broadcasted_iota(jnp.int32, (1, TILE * ROWS), 1)
    start = jnp.zeros((1, TILE * ROWS), jnp.int32)
    first = jnp.int32(0)
    end = jnp.int32(0)
    for j in range(docs):
        end = end + len_ref[0, j]
        start = jnp.where(token >= end, end, start)
        first = jnp.where(base >= end, end, first)
    needed = step * TILE - first // ROWS + TILE

    def block(count):
        width = count * ROWS
        key_at = pl.multiple_of((step * TILE + TILE - count) * ROWS, ROWS)
        window = pl.ds(key_at, width)
        mine = pl.ds(pl.multiple_of(base, TILE * ROWS), TILE * ROWS)
        recip = jnp.concatenate(
            [column(recip_ref[pl.ds(step * TILE + n, 1), :]) for n in range(TILE)], axis=0
        )
        key = key_at + lax.broadcasted_iota(jnp.int32, (width, TILE * ROWS), 0)
        bias = jnp.where((key >= start) & (key <= token), 0.0, big_negative)
        keys = kn_ref[window, :]
        values = v_ref[window, :]
        keys_t = kn_t_ref[:, window]

        def products(h):
            lanes = slice(h * HDIM, (h + 1) * HDIM)
            tile = q_ref[:, lanes].astype(jnp.float32) * recip * q_gain_ref[:, lanes]
            queries = tile.astype(jnp.bfloat16)
            grads = grad_ref[:, lanes]
            return queries, grads, nt_dot(keys, queries), nt_dot(values, grads)

        def softmax(h, scores, upper):
            logits = scores * (scaling * math.log2(math.e)) + bias
            peak = jnp.max(logits, axis=0, keepdims=True)
            powers = jnp.exp2(logits - peak)
            total = jnp.sum(powers, axis=0, keepdims=True)
            lse_ref[h : h + 1, mine] = peak * math.log(2.0) + jnp.log(total)
            weights = powers * (1.0 / total)
            low = weights.astype(jnp.bfloat16)
            delta = jnp.sum(low.astype(jnp.float32) * upper, axis=0, keepdims=True)
            return low, (weights * (upper - delta) * scaling).astype(jnp.bfloat16)

        def gradients(h, queries, grads, weights_low, grad_low):
            lanes = slice(h * HDIM, (h + 1) * HDIM)
            dv = jnp.dot(weights_low, grads, preferred_element_type=jnp.float32)
            dk = jnp.dot(grad_low, queries, preferred_element_type=jnp.float32)
            dq_t = jnp.dot(keys_t, grad_low, preferred_element_type=jnp.float32)
            low = jnp.transpose(dq_t).astype(jnp.bfloat16)
            dq_ref[:, lanes] = low
            inner = (
                low.astype(jnp.float32)
                * q_gain_ref[:, lanes]
                * q_ref[:, lanes].astype(jnp.float32)
            )
            return dv, dk, inner

        ready = [products(0)]
        inner = jnp.zeros((TILE * ROWS, HDIM), jnp.float32)
        for h in range(heads):
            if h + 1 < heads:
                ready.append(products(h + 1))
            queries, grads, scores, upper = ready[h]
            weights_low, grad_low = softmax(h, scores, upper)
            dv, dk, term = gradients(h, queries, grads, weights_low, grad_low)
            dv_acc[window, :] += dv
            dk_acc[window, :] += dk
            inner += term
        for n in range(TILE):
            back_ref[pl.ds(step * TILE + n, 1), :] = row_sums(inner[n * ROWS : (n + 1) * ROWS])

    for count in range(TILE, REACH // ROWS + TILE + 1):
        pl.when(needed == count)(functools.partial(block, count))

    @pl.when(step == pl.num_programs(0) - 1)
    def _():
        dv_ref[...] = dv_acc[...].astype(jnp.bfloat16)
        for b in range(blocks):
            at = slice(b * ROWS, (b + 1) * ROWS)
            low = dk_acc[at, :].astype(jnp.bfloat16)
            dk_ref[at, :] = low
            back_ref[blocks + b : blocks + b + 1, :] = row_sums(
                low.astype(jnp.float32) * k_gain_ref[...] * k_ref[at, :].astype(jnp.float32)
            )
        slots_ref[...] = jnp.zeros_like(slots_ref)
        logs = lse_ref[...]
        home = jnp.zeros((8, home_count), jnp.float32)
        kept = jnp.int32(0)
        begin = jnp.int32(0)
        home_at = lax.broadcasted_iota(jnp.int32, (8, home_count), 1)
        for j in range(docs):
            length = len_ref[0, j]
            dest = dest_ref[0, j]
            stays = dest == here
            shift = jnp.where(stays, kept, off_ref[0, j])
            turned = pltpu.roll(logs, lax.rem(shift - begin + seq_len, seq_len), 1)
            inside = (home_at >= shift) & (home_at < shift + length)
            piece = jnp.where(inside, turned[:, :home_count], 0.0)
            home += jnp.where(stays, piece, 0.0)

            @pl.when(jnp.logical_not(stays))
            def _():
                slots_ref[dest] = piece[:, :slot]

            kept = kept + jnp.where(stays, length, 0)
            begin = begin + length
        home_ref[...] = home


def attention(q, k, v, d_out, recip, q_gain, k_gain, lengths, dest, offset, devices, slot):
    seq_len, width = q.shape
    blocks = seq_len // ROWS
    home_count = seq_len // 4
    smem = pl.BlockSpec(memory_space=pltpu.SMEM)

    def whole(shape):
        return pl.BlockSpec(shape, lambda i: (0,) * len(shape))

    rows = pl.BlockSpec((ROWS * TILE, width), lambda i: (i, 0))
    kv = whole((seq_len, HDIM))
    return pl.pallas_call(
        functools.partial(attention_kernel, lengths.shape[1], devices, slot, home_count),
        grid=(blocks // TILE,),
        in_specs=[
            smem,
            smem,
            smem,
            rows,
            rows,
            kv,
            pl.BlockSpec(memory_space=pltpu.HBM),
            whole((2 * blocks, ROWS)),
            whole((1, width)),
            whole((1, HDIM)),
        ],
        out_specs=[
            rows,
            kv,
            kv,
            whole((2 * blocks, ROWS)),
            whole((8, home_count)),
            whole((devices, 8, slot)),
        ],
        out_shape=[
            jax.ShapeDtypeStruct((seq_len, width), jnp.bfloat16),
            jax.ShapeDtypeStruct((seq_len, HDIM), jnp.bfloat16),
            jax.ShapeDtypeStruct((seq_len, HDIM), jnp.bfloat16),
            jax.ShapeDtypeStruct((2 * blocks, ROWS), jnp.float32),
            jax.ShapeDtypeStruct((8, home_count), jnp.float32),
            jax.ShapeDtypeStruct((devices, 8, slot), jnp.float32),
        ],
        scratch_shapes=[
            pltpu.VMEM((seq_len, HDIM), jnp.bfloat16),
            pltpu.VMEM((HDIM, seq_len), jnp.bfloat16),
            pltpu.VMEM((seq_len, HDIM), jnp.float32),
            pltpu.VMEM((seq_len, HDIM), jnp.float32),
            pltpu.VMEM((8, seq_len), jnp.float32),
            pltpu.VMEM((seq_len, HDIM), jnp.bfloat16),
            pltpu.SemaphoreType.DMA,
        ],
        compiler_params=pltpu.CompilerParams(
            vmem_limit_bytes=61 * 1024 * 1024, dimension_semantics=("arbitrary",)
        ),
        cost_estimate=pl.CostEstimate(
            flops=10 * seq_len * REACH * width,
            bytes_accessed=8 * seq_len * width,
            transcendentals=seq_len * REACH * width // HDIM,
        ),
    )(lengths, dest, offset, q, d_out, k, v, recip, q_gain, k_gain)


def peer_sum(parts_ref, got_ref, send_sem, recv_sem, me, peers):
    copies = []
    for d in range(1, peers):
        copy = pltpu.make_async_remote_copy(
            src_ref=parts_ref,
            dst_ref=got_ref.at[d - 1],
            send_sem=send_sem.at[d - 1],
            recv_sem=recv_sem.at[d - 1],
            device_id={"head": lax.rem(me + d, peers)},
            device_id_type=pl.DeviceIdType.MESH,
        )
        copy.start()
        copies.append(copy)
    return copies


def stat_kernel(
    peers, q_hbm, k_hbm, recip_ref, q_ref, k_ref, parts_ref, got_ref, send_sem, recv_sem, load_sem
):
    me = lax.axis_index("head")
    seq_len, width = q_ref.shape
    blocks = seq_len // ROWS
    part = seq_len // CHUNKS
    loads = [pltpu.make_async_copy(k_hbm, k_ref, load_sem.at[CHUNKS])]
    for c in range(CHUNKS):
        at = pl.ds(c * part, part)
        loads.append(pltpu.make_async_copy(q_hbm.at[at], q_ref.at[at], load_sem.at[c]))
    for load in loads:
        load.start()
    barrier = pltpu.get_barrier_semaphore()
    for d in range(1, peers):
        pl.semaphore_signal(
            barrier,
            inc=1,
            device_id={"head": lax.rem(me + d, peers)},
            device_id_type=pl.DeviceIdType.MESH,
        )
    loads[0].wait()
    for b in range(blocks):
        at = slice(b * ROWS, (b + 1) * ROWS)
        tile = k_ref[at, :].astype(jnp.float32)
        parts_ref[blocks + b : blocks + b + 1, :] = row_sums(tile * tile)
    for b in range(blocks):
        if b % (blocks // CHUNKS) == 0:
            loads[1 + b // (blocks // CHUNKS)].wait()
        at = slice(b * ROWS, (b + 1) * ROWS)
        total = jnp.zeros((ROWS, HDIM), jnp.float32)
        for h in range(width // HDIM):
            tile = q_ref[at, h * HDIM : (h + 1) * HDIM].astype(jnp.float32)
            total += tile * tile
        parts_ref[b : b + 1, :] = row_sums(total)
    pl.semaphore_wait(barrier, peers - 1)
    copies = peer_sum(parts_ref, got_ref, send_sem, recv_sem, me, peers)
    for copy in copies:
        copy.wait()
    sums = parts_ref[...]
    for d in range(peers - 1):
        sums += got_ref[d]
    recip_ref[:blocks, :] = lax.rsqrt(sums[:blocks] / (width * peers) + eps)
    recip_ref[blocks:, :] = lax.rsqrt(sums[blocks:] / (HDIM * peers) + eps)


def token_scales(q, k, peers):
    blocks = q.shape[0] // ROWS
    vmem = pl.BlockSpec(memory_space=pltpu.VMEM)
    return pl.pallas_call(
        functools.partial(stat_kernel, peers),
        out_shape=jax.ShapeDtypeStruct((2 * blocks, ROWS), jnp.float32),
        in_specs=[pl.BlockSpec(memory_space=pltpu.HBM)] * 2,
        out_specs=vmem,
        scratch_shapes=[
            pltpu.VMEM(q.shape, q.dtype),
            pltpu.VMEM(k.shape, k.dtype),
            pltpu.VMEM((2 * blocks, ROWS), jnp.float32),
            pltpu.VMEM((peers - 1, 2 * blocks, ROWS), jnp.float32),
            pltpu.SemaphoreType.DMA((peers - 1,)),
            pltpu.SemaphoreType.DMA((peers - 1,)),
            pltpu.SemaphoreType.DMA((CHUNKS + 1,)),
        ],
        compiler_params=pltpu.CompilerParams(
            collective_id=0, has_side_effects=True, vmem_limit_bytes=63 * 1024 * 1024
        ),
    )(q, k)


def finish_kernel(
    peers,
    devices,
    width_q,
    recip_hbm,
    back_hbm,
    slots_ref,
    cube_ref,
    logs_ref,
    got_ref,
    log_got_ref,
    send_sem,
    recv_sem,
    log_send_sem,
    log_recv_sem,
    recip_ref,
    back_ref,
    load_sem,
):
    me = lax.axis_index("head")
    here = lax.axis_index("dp")
    blocks = back_ref.shape[0] // 2
    load_back = pltpu.make_async_copy(back_hbm, back_ref, load_sem.at[0])
    load_recip = pltpu.make_async_copy(recip_hbm, recip_ref, load_sem.at[1])
    load_back.start()
    load_recip.start()
    barrier = pltpu.get_barrier_semaphore()
    for d in range(1, peers):
        pl.semaphore_signal(
            barrier,
            inc=1,
            device_id={"head": lax.rem(me + d, peers)},
            device_id_type=pl.DeviceIdType.MESH,
        )
    for d in range(1, devices):
        pl.semaphore_signal(
            barrier,
            inc=1,
            device_id={"dp": lax.rem(here + d, devices)},
            device_id_type=pl.DeviceIdType.MESH,
        )
    load_back.wait()
    load_recip.wait()
    pl.semaphore_wait(barrier, peers - 1 + devices - 1)
    copies = peer_sum(back_ref, got_ref, send_sem, recv_sem, me, peers)
    log_copies = []
    for d in range(1, devices):
        there = lax.rem(here + d, devices)
        copy = pltpu.make_async_remote_copy(
            src_ref=slots_ref.at[there],
            dst_ref=log_got_ref.at[here],
            send_sem=log_send_sem.at[d - 1],
            recv_sem=log_recv_sem.at[d - 1],
            device_id={"dp": there},
            device_id_type=pl.DeviceIdType.MESH,
        )
        copy.start()
        log_copies.append(copy)
    for copy in copies:
        copy.wait()
    sums = back_ref[...]
    for d in range(peers - 1):
        sums += got_ref[d]
    recip = recip_ref[...]
    cubes = recip * recip * recip * sums
    cube_ref[:blocks, :] = cubes[:blocks] / width_q
    cube_ref[blocks:, :] = cubes[blocks:] / (HDIM * peers)
    for copy in log_copies:
        copy.wait()
    log_got_ref[here] = jnp.zeros(log_got_ref.shape[1:], jnp.float32)
    logs_ref[...] = log_got_ref[...]


def finish(recip, back, slots, peers, width):
    devices, pad, slot = slots.shape
    vmem = pl.BlockSpec(memory_space=pltpu.VMEM)
    return pl.pallas_call(
        functools.partial(finish_kernel, peers, devices, width * peers),
        out_shape=[
            jax.ShapeDtypeStruct(back.shape, jnp.float32),
            jax.ShapeDtypeStruct(slots.shape, jnp.float32),
        ],
        in_specs=[pl.BlockSpec(memory_space=pl.ANY)] * 3,
        out_specs=[vmem, vmem],
        scratch_shapes=[
            pltpu.VMEM((peers - 1,) + back.shape, jnp.float32),
            pltpu.VMEM(slots.shape, jnp.float32),
            pltpu.SemaphoreType.DMA((peers - 1,)),
            pltpu.SemaphoreType.DMA((peers - 1,)),
            pltpu.SemaphoreType.DMA((devices - 1,)),
            pltpu.SemaphoreType.DMA((devices - 1,)),
            pltpu.VMEM(back.shape, jnp.float32),
            pltpu.VMEM(back.shape, jnp.float32),
            pltpu.SemaphoreType.DMA((2,)),
        ],
        compiler_params=pltpu.CompilerParams(
            collective_id=1, has_side_effects=True, vmem_limit_bytes=32 * 1024 * 1024
        ),
    )(recip, back, slots)


def local(q_raw, k_raw, v_proj, d_out, q_gain, k_gain, doc_lengths, plan_dest, plan_offset):
    seq_len = q_raw.shape[0]
    heads = q_raw.shape[1] // HDIM
    blocks = seq_len // ROWS
    devices = lax.axis_size("dp")
    peers = lax.axis_size("head")
    span = 2 * seq_len
    slot = span // devices
    recip = token_scales(q_raw, k_raw, peers)
    dq_norm, dk_norm, grad_v, back, home_log, slots = attention(
        q_raw,
        k_raw,
        v_proj,
        d_out,
        recip,
        q_gain.reshape(1, -1),
        k_gain.reshape(1, -1),
        doc_lengths,
        plan_dest,
        plan_offset,
        devices,
        slot,
    )
    cubes, got = finish(recip, back, slots, peers, q_raw.shape[1])
    away_log = jnp.transpose(got[:, :heads, :], (1, 0, 2)).reshape(heads, span)
    balanced = jnp.concatenate([home_log[:heads], away_log], axis=1)
    recip = recip.reshape(2, seq_len)
    cubes = cubes.reshape(2, seq_len)
    scaled_q = dq_norm.astype(jnp.float32) * q_gain[None, :]
    scaled_k = dk_norm.astype(jnp.float32) * k_gain[None, :]
    q_float = q_raw.astype(jnp.float32)
    k_float = k_raw.astype(jnp.float32)
    grad_q = (recip[0][:, None] * scaled_q - q_float * cubes[0][:, None]).astype(jnp.bfloat16)
    grad_k = (recip[1][:, None] * scaled_k - k_float * cubes[1][:, None]).astype(jnp.bfloat16)
    return (grad_q, grad_k, grad_v, balanced)


def solution(mesh):
    in_specs = (
        P("dp", "head"),
        P("dp", "head"),
        P("dp", "head"),
        P("dp", "head"),
        P("head"),
        P("head"),
        P("dp", None),
        P("dp", None),
        P("dp", None),
    )
    out_specs = (P("dp", "head"), P("dp", "head"), P("dp", "head"), P("head", "dp"))
    return jax.shard_map(local, mesh=mesh, in_specs=in_specs, out_specs=out_specs, check_vma=False)
```

```python
import functools
import math

import jax
import jax.numpy as jnp
from jax import lax
from jax.experimental import pallas as pl
from jax.experimental.pallas import tpu as pltpu
from jax.sharding import PartitionSpec as P

HDIM = 128
ROWS = 128
REACH = 384
STEP_BLOCKS = 3

eps = 1e-06
big_negative = -1e30


def column(row):
    return jnp.transpose(jnp.broadcast_to(row, (ROWS, ROWS)))


def row_sums(tile):
    return jnp.sum(jnp.transpose(tile), axis=0, keepdims=True)


def nt_dot(a, b):
    return lax.dot_general(a, b, (((1,), (1,)), ((), ())), preferred_element_type=jnp.float32)


def attention_kernel(
    docs,
    devices,
    slot,
    home_count,
    len_ref,
    dest_ref,
    off_ref,
    q_ref,
    grad_ref,
    k_ref,
    v_ref,
    recip_ref,
    q_gain_ref,
    k_gain_ref,
    dq_ref,
    dk_ref,
    dv_ref,
    back_ref,
    home_ref,
    slots_ref,
    kn_ref,
    kn_t_ref,
    dk_acc,
    dv_acc,
    lse_ref,
):
    step = pl.program_id(0)
    seq_len = k_ref.shape[0]
    blocks = seq_len // ROWS
    heads = q_ref.shape[1] // HDIM
    scaling = 1.0 / math.sqrt(HDIM)
    here = lax.axis_index("dp")

    @pl.when(step == 0)
    def _():
        dk_acc[...] = jnp.zeros_like(dk_acc)
        dv_acc[...] = jnp.zeros_like(dv_acc)
        lse_ref[...] = jnp.zeros_like(lse_ref)
        for b in range(blocks):
            at = slice(b * ROWS, (b + 1) * ROWS)
            normed = (
                k_ref[at, :].astype(jnp.float32)
                * column(recip_ref[blocks + b : blocks + b + 1, :])
                * k_gain_ref[...]
            )
            low = normed.astype(jnp.bfloat16)
            kn_ref[at, :] = low
            kn_t_ref[:, at] = jnp.transpose(low.astype(jnp.float32)).astype(jnp.bfloat16)

    def block(index, start, token, count):
        width = count * ROWS
        key_at = pl.multiple_of((index - (count - 1)) * ROWS, ROWS)
        window = pl.ds(key_at, width)
        here_at = pl.multiple_of(index * ROWS, ROWS)
        mine = pl.ds(pl.multiple_of(lax.rem(index, STEP_BLOCKS) * ROWS, ROWS), ROWS)
        recip = column(recip_ref[pl.ds(index, 1), :])
        key = key_at + lax.broadcasted_iota(jnp.int32, (width, ROWS), 0)
        bias = jnp.where((key >= start) & (key <= token), 0.0, big_negative)
        keys = kn_ref[window, :]
        values = v_ref[window, :]
        keys_t = kn_t_ref[:, window]

        def products(group):
            normed, upstream = [], []
            for h in group:
                lanes = slice(h * HDIM, (h + 1) * HDIM)
                tile = q_ref[mine, lanes].astype(jnp.float32) * recip * q_gain_ref[:, lanes]
                normed.append(tile.astype(jnp.bfloat16))
                upstream.append(grad_ref[mine, lanes])
            queries = jnp.concatenate(normed, axis=0)
            grads = jnp.concatenate(upstream, axis=0)
            return queries, grads, nt_dot(keys, queries), nt_dot(values, grads)

        def softmax(group, scores, grad_weights):
            weights_all, grad_all = [], []
            for n, h in enumerate(group):
                lanes = slice(n * HDIM, (n + 1) * HDIM)
                logits = scores[:, lanes] * (scaling * math.log2(math.e)) + bias
                peak = jnp.max(logits, axis=0, keepdims=True)
                powers = jnp.exp2(logits - peak)
                total = jnp.sum(powers, axis=0, keepdims=True)
                lse_ref[h : h + 1, pl.ds(here_at, ROWS)] = peak * math.log(2.0) + jnp.log(total)
                weights = powers * (1.0 / total)
                low = weights.astype(jnp.bfloat16)
                upper = grad_weights[:, lanes]
                delta = jnp.sum(low.astype(jnp.float32) * upper, axis=0, keepdims=True)
                weights_all.append(low)
                grad_all.append((weights * (upper - delta) * scaling).astype(jnp.bfloat16))
            return jnp.concatenate(weights_all, axis=1), jnp.concatenate(grad_all, axis=1)

        def gradients(group, queries, grads, weights_low, grad_low):
            dv = jnp.dot(weights_low, grads, preferred_element_type=jnp.float32)
            dk = jnp.dot(grad_low, queries, preferred_element_type=jnp.float32)
            dq_t = jnp.dot(keys_t, grad_low, preferred_element_type=jnp.float32)
            inner = jnp.zeros((ROWS, HDIM), jnp.float32)
            for n, h in enumerate(group):
                lanes = slice(h * HDIM, (h + 1) * HDIM)
                low = jnp.transpose(dq_t[:, n * HDIM : (n + 1) * HDIM]).astype(jnp.bfloat16)
                dq_ref[mine, lanes] = low
                inner += (
                    low.astype(jnp.float32)
                    * q_gain_ref[:, lanes]
                    * q_ref[mine, lanes].astype(jnp.float32)
                )
            return dv, dk, inner

        groups = [range(h, min(h + 2, heads)) for h in range(0, heads, 2)]
        ready = [products(groups[0])]
        results = []
        for n, group in enumerate(groups):
            if n + 1 < len(groups):
                ready.append(products(groups[n + 1]))
            queries, grads, scores, grad_weights = ready[n]
            weights_low, grad_low = softmax(group, scores, grad_weights)
            results.append(gradients(group, queries, grads, weights_low, grad_low))
        dv_acc[window, :] += sum(r[0] for r in results)
        dk_acc[window, :] += sum(r[1] for r in results)
        back_ref[pl.ds(index, 1), :] = row_sums(sum(r[2] for r in results))

    @pl.loop(0, STEP_BLOCKS)
    def _(part):
        index = step * STEP_BLOCKS + part
        base = index * ROWS
        token = base + lax.broadcasted_iota(jnp.int32, (1, ROWS), 1)
        start = jnp.zeros((1, ROWS), jnp.int32)
        first = jnp.int32(0)
        end = jnp.int32(0)
        for j in range(docs):
            end = end + len_ref[0, j]
            start = jnp.where(token >= end, end, start)
            first = jnp.where(base >= end, end, first)
        needed = index - first // ROWS + 1
        for count in range(1, REACH // ROWS + 2):
            pl.when(needed == count)(functools.partial(block, index, start, token, count))

    @pl.when(step == pl.num_programs(0) - 1)
    def _():
        dv_ref[...] = dv_acc[...].astype(jnp.bfloat16)
        for b in range(blocks):
            at = slice(b * ROWS, (b + 1) * ROWS)
            low = dk_acc[at, :].astype(jnp.bfloat16)
            dk_ref[at, :] = low
            back_ref[blocks + b : blocks + b + 1, :] = row_sums(
                low.astype(jnp.float32) * k_gain_ref[...] * k_ref[at, :].astype(jnp.float32)
            )
        slots_ref[...] = jnp.zeros_like(slots_ref)
        logs = lse_ref[...]
        home = jnp.zeros((8, home_count), jnp.float32)
        kept = jnp.int32(0)
        begin = jnp.int32(0)
        home_at = lax.broadcasted_iota(jnp.int32, (8, home_count), 1)
        for j in range(docs):
            length = len_ref[0, j]
            dest = dest_ref[0, j]
            stays = dest == here
            shift = jnp.where(stays, kept, off_ref[0, j])
            turned = pltpu.roll(logs, lax.rem(shift - begin + seq_len, seq_len), 1)
            inside = (home_at >= shift) & (home_at < shift + length)
            piece = jnp.where(inside, turned[:, :home_count], 0.0)
            home += jnp.where(stays, piece, 0.0)

            @pl.when(jnp.logical_not(stays))
            def _():
                slots_ref[dest] = piece[:, :slot]

            kept = kept + jnp.where(stays, length, 0)
            begin = begin + length
        home_ref[...] = home


def attention(q, k, v, d_out, recip, q_gain, k_gain, lengths, dest, offset, devices, slot):
    seq_len, width = q.shape
    blocks = seq_len // ROWS
    home_count = seq_len // 4
    smem = pl.BlockSpec(memory_space=pltpu.SMEM)

    def whole(shape):
        return pl.BlockSpec(shape, lambda i: (0,) * len(shape))

    rows = pl.BlockSpec((ROWS * STEP_BLOCKS, width), lambda i: (i, 0))
    kv = whole((seq_len, HDIM))
    return pl.pallas_call(
        functools.partial(attention_kernel, lengths.shape[1], devices, slot, home_count),
        grid=(blocks // STEP_BLOCKS,),
        in_specs=[
            smem,
            smem,
            smem,
            rows,
            rows,
            kv,
            kv,
            whole((2 * blocks, ROWS)),
            whole((1, width)),
            whole((1, HDIM)),
        ],
        out_specs=[
            rows,
            kv,
            kv,
            whole((2 * blocks, ROWS)),
            whole((8, home_count)),
            whole((devices, 8, slot)),
        ],
        out_shape=[
            jax.ShapeDtypeStruct((seq_len, width), jnp.bfloat16),
            jax.ShapeDtypeStruct((seq_len, HDIM), jnp.bfloat16),
            jax.ShapeDtypeStruct((seq_len, HDIM), jnp.bfloat16),
            jax.ShapeDtypeStruct((2 * blocks, ROWS), jnp.float32),
            jax.ShapeDtypeStruct((8, home_count), jnp.float32),
            jax.ShapeDtypeStruct((devices, 8, slot), jnp.float32),
        ],
        scratch_shapes=[
            pltpu.VMEM((seq_len, HDIM), jnp.bfloat16),
            pltpu.VMEM((HDIM, seq_len), jnp.bfloat16),
            pltpu.VMEM((seq_len, HDIM), jnp.float32),
            pltpu.VMEM((seq_len, HDIM), jnp.float32),
            pltpu.VMEM((8, seq_len), jnp.float32),
        ],
        compiler_params=pltpu.CompilerParams(
            vmem_limit_bytes=48 * 1024 * 1024, dimension_semantics=("arbitrary",)
        ),
        cost_estimate=pl.CostEstimate(
            flops=10 * seq_len * REACH * width,
            bytes_accessed=8 * seq_len * width,
            transcendentals=seq_len * REACH * width // HDIM,
        ),
    )(lengths, dest, offset, q, d_out, k, v, recip, q_gain, k_gain)


def peer_sum(parts_ref, got_ref, send_sem, recv_sem, me, peers):
    copies = []
    for d in range(1, peers):
        copy = pltpu.make_async_remote_copy(
            src_ref=parts_ref,
            dst_ref=got_ref.at[d - 1],
            send_sem=send_sem.at[d - 1],
            recv_sem=recv_sem.at[d - 1],
            device_id={"head": lax.rem(me + d, peers)},
            device_id_type=pl.DeviceIdType.MESH,
        )
        copy.start()
        copies.append(copy)
    return copies


def stat_kernel(peers, q_ref, k_ref, recip_ref, parts_ref, got_ref, send_sem, recv_sem):
    me = lax.axis_index("head")
    seq_len, width = q_ref.shape
    blocks = seq_len // ROWS
    barrier = pltpu.get_barrier_semaphore()
    for d in range(1, peers):
        pl.semaphore_signal(
            barrier,
            inc=1,
            device_id={"head": lax.rem(me + d, peers)},
            device_id_type=pl.DeviceIdType.MESH,
        )
    for b in range(blocks):
        at = slice(b * ROWS, (b + 1) * ROWS)
        total = jnp.zeros((ROWS, HDIM), jnp.float32)
        for h in range(width // HDIM):
            tile = q_ref[at, h * HDIM : (h + 1) * HDIM].astype(jnp.float32)
            total += tile * tile
        parts_ref[b : b + 1, :] = row_sums(total)
        tile = k_ref[at, :].astype(jnp.float32)
        parts_ref[blocks + b : blocks + b + 1, :] = row_sums(tile * tile)
    pl.semaphore_wait(barrier, peers - 1)
    copies = peer_sum(parts_ref, got_ref, send_sem, recv_sem, me, peers)
    for copy in copies:
        copy.wait()
    sums = parts_ref[...]
    for d in range(peers - 1):
        sums += got_ref[d]
    recip_ref[:blocks, :] = lax.rsqrt(sums[:blocks] / (width * peers) + eps)
    recip_ref[blocks:, :] = lax.rsqrt(sums[blocks:] / (HDIM * peers) + eps)


def token_scales(q, k, peers):
    blocks = q.shape[0] // ROWS
    vmem = pl.BlockSpec(memory_space=pltpu.VMEM)
    return pl.pallas_call(
        functools.partial(stat_kernel, peers),
        out_shape=jax.ShapeDtypeStruct((2 * blocks, ROWS), jnp.float32),
        in_specs=[vmem, vmem],
        out_specs=vmem,
        scratch_shapes=[
            pltpu.VMEM((2 * blocks, ROWS), jnp.float32),
            pltpu.VMEM((peers - 1, 2 * blocks, ROWS), jnp.float32),
            pltpu.SemaphoreType.DMA((peers - 1,)),
            pltpu.SemaphoreType.DMA((peers - 1,)),
        ],
        compiler_params=pltpu.CompilerParams(
            collective_id=0, has_side_effects=True, vmem_limit_bytes=32 * 1024 * 1024
        ),
    )(q, k)


def finish_kernel(
    peers,
    devices,
    width_q,
    recip_ref,
    back_ref,
    slots_ref,
    cube_ref,
    logs_ref,
    got_ref,
    log_got_ref,
    send_sem,
    recv_sem,
    log_send_sem,
    log_recv_sem,
):
    me = lax.axis_index("head")
    here = lax.axis_index("dp")
    rows = back_ref.shape[0]
    blocks = rows // 2
    barrier = pltpu.get_barrier_semaphore()
    for d in range(1, peers):
        pl.semaphore_signal(
            barrier,
            inc=1,
            device_id={"head": lax.rem(me + d, peers)},
            device_id_type=pl.DeviceIdType.MESH,
        )
    for d in range(1, devices):
        pl.semaphore_signal(
            barrier,
            inc=1,
            device_id={"dp": lax.rem(here + d, devices)},
            device_id_type=pl.DeviceIdType.MESH,
        )
    pl.semaphore_wait(barrier, peers - 1 + devices - 1)
    copies = peer_sum(back_ref, got_ref, send_sem, recv_sem, me, peers)
    log_copies = []
    for d in range(1, devices):
        there = lax.rem(here + d, devices)
        copy = pltpu.make_async_remote_copy(
            src_ref=slots_ref.at[there],
            dst_ref=log_got_ref.at[here],
            send_sem=log_send_sem.at[d - 1],
            recv_sem=log_recv_sem.at[d - 1],
            device_id={"dp": there},
            device_id_type=pl.DeviceIdType.MESH,
        )
        copy.start()
        log_copies.append(copy)
    for copy in copies:
        copy.wait()
    sums = back_ref[...]
    for d in range(peers - 1):
        sums += got_ref[d]
    recip = recip_ref[...]
    cubes = recip * recip * recip * sums
    cube_ref[:blocks, :] = cubes[:blocks] / width_q
    cube_ref[blocks:, :] = cubes[blocks:] / (HDIM * peers)
    for copy in log_copies:
        copy.wait()
    log_got_ref[here] = jnp.zeros(log_got_ref.shape[1:], jnp.float32)
    logs_ref[...] = log_got_ref[...]


def finish(recip, back, slots, peers, width):
    devices, pad, slot = slots.shape
    vmem = pl.BlockSpec(memory_space=pltpu.VMEM)
    return pl.pallas_call(
        functools.partial(finish_kernel, peers, devices, width * peers),
        out_shape=[
            jax.ShapeDtypeStruct(back.shape, jnp.float32),
            jax.ShapeDtypeStruct(slots.shape, jnp.float32),
        ],
        in_specs=[vmem, vmem, vmem],
        out_specs=[vmem, vmem],
        scratch_shapes=[
            pltpu.VMEM((peers - 1,) + back.shape, jnp.float32),
            pltpu.VMEM(slots.shape, jnp.float32),
            pltpu.SemaphoreType.DMA((peers - 1,)),
            pltpu.SemaphoreType.DMA((peers - 1,)),
            pltpu.SemaphoreType.DMA((devices - 1,)),
            pltpu.SemaphoreType.DMA((devices - 1,)),
        ],
        compiler_params=pltpu.CompilerParams(
            collective_id=1, has_side_effects=True, vmem_limit_bytes=32 * 1024 * 1024
        ),
    )(recip, back, slots)


def local(q_raw, k_raw, v_proj, d_out, q_gain, k_gain, doc_lengths, plan_dest, plan_offset):
    seq_len = q_raw.shape[0]
    heads = q_raw.shape[1] // HDIM
    blocks = seq_len // ROWS
    devices = lax.axis_size("dp")
    peers = lax.axis_size("head")
    span = 2 * seq_len
    slot = span // devices
    recip = token_scales(q_raw, k_raw, peers)
    dq_norm, dk_norm, grad_v, back, home_log, slots = attention(
        q_raw,
        k_raw,
        v_proj,
        d_out,
        recip,
        q_gain.reshape(1, -1),
        k_gain.reshape(1, -1),
        doc_lengths,
        plan_dest,
        plan_offset,
        devices,
        slot,
    )
    cubes, got = finish(recip, back, slots, peers, q_raw.shape[1])
    away_log = jnp.transpose(got[:, :heads, :], (1, 0, 2)).reshape(heads, span)
    balanced = jnp.concatenate([home_log[:heads], away_log], axis=1)
    recip = recip.reshape(2, seq_len)
    cubes = cubes.reshape(2, seq_len)
    scaled_q = dq_norm.astype(jnp.float32) * q_gain[None, :]
    scaled_k = dk_norm.astype(jnp.float32) * k_gain[None, :]
    q_float = q_raw.astype(jnp.float32)
    k_float = k_raw.astype(jnp.float32)
    grad_q = (recip[0][:, None] * scaled_q - q_float * cubes[0][:, None]).astype(jnp.bfloat16)
    grad_k = (recip[1][:, None] * scaled_k - k_float * cubes[1][:, None]).astype(jnp.bfloat16)
    return (grad_q, grad_k, grad_v, balanced)


def solution(mesh):
    in_specs = (
        P("dp", "head"),
        P("dp", "head"),
        P("dp", "head"),
        P("dp", "head"),
        P("head"),
        P("head"),
        P("dp", None),
        P("dp", None),
        P("dp", None),
    )
    out_specs = (P("dp", "head"), P("dp", "head"), P("dp", "head"), P("head", "dp"))
    return jax.shard_map(local, mesh=mesh, in_specs=in_specs, out_specs=out_specs, check_vma=False)
```
